512 devices in a mesh: section: 64 (over z, y_lo, core), tensor: 8 (over x, y_hi).
Axes of the slice: x: 4, y: 4 (y_hi: 2, y_lo: 2; y = y_hi * 2 + y_lo), z: 16, core: 2. Of those that a mesh axis runs over, the one named last changes fastest.
Arguments:
- activations: bfloat16 [256, 8192], P(None, 'tensor'), may hold values from -6 to 6
- cotangent: bfloat16 [256, 8192], P(None, 'tensor'), may hold values from -6 to 6
- up_weight: bfloat16 [2, 8192, 28672], P(None, 'tensor', 'section'), may hold values from -0.0625 to 0.0625
- down_weight: bfloat16 [2, 28672, 8192], P(None, 'section', 'tensor'), may hold values from -0.03125 to 0.03125
- width_proj: bfloat16 [64, 8192], P(None, 'tensor'), may hold values from -0.0625 to 0.0625
- hidden_proj: bfloat16 [64, 28672], P(None, 'section'), may hold values from -0.0625 to 0.0625
- queries: bfloat16 [512, 16384], P('tensor', 'section'), may hold values from -0.03125 to 0.03125
Outputs:
- scores: float32 [2, 512], P(None, 'tensor')
- input_grad: bfloat16 [256, 8192], P('section', 'tensor')
The draws below stay inside these ranges and needn't reach their ends.
All inputs are finite; a program needn't handle non-finite values.
Results may differ from the reference program's by a relative error of at most 0.03.
Values may be sent and summed in bfloat16 or wider, within the bound.
A program may use at most 64 MiB of HBM per device.

```python
import jax
import jax.numpy as jnp
from jax import lax

D = 8192
FF = 28672
K = 64
LAYERS = 2
EX = 2
LEN = 128
NQ = 512
TOK = 256
MATS = 4
N_TENSOR = 8


def with_spikes(values, key, source, target, blocks, factor):
    def block_of(dim):
        return (jnp.arange(values.shape[dim]) // (values.shape[dim] // blocks)).reshape((-1,) + (1,) * (values.ndim - 1 - dim))

    first = jax.random.permutation(key, blocks)[block_of(target)]
    far = (block_of(target) + blocks // 2) % blocks
    return jnp.where((block_of(source) == first) | (block_of(source) == far), factor * values, values)


def block_scale(key, shape, cuts, smallest, high):
    def one(axis_at, shards_of):
        steps = jax.random.uniform(jax.random.fold_in(jax.random.fold_in(key, 6), axis_at), (shards_of,), jnp.float32, smallest / len(cuts), high / len(cuts))
        return jnp.repeat(jnp.exp(steps), shape[axis_at] // shards_of).reshape((-1,) + (1,) * (len(shape) - axis_at - 1))

    loudness = one(*cuts[0])
    for cut in cuts[1:]:
        loudness = loudness * one(*cut)
    return loudness


def bell_draw(rng, dims, spread, limit, pieces=(), dtype=jnp.bfloat16):
    drawn = jax.random.normal(rng, dims, jnp.float32) * spread
    if len(pieces) > 0:
        drawn = block_scale(rng, dims, pieces, -0.22, 0.18) * drawn
    return jnp.clip(drawn, min=-limit, max=limit).astype(dtype)


def bell_draw_with(rng, dims, spread, reach, cuts, heavy, dtype=jnp.bfloat16):
    drawn = spread * jax.random.normal(rng, dims, jnp.float32)
    if cuts:
        drawn = drawn * block_scale(rng, dims, cuts, -0.22, 0.18)
    return jnp.clip(with_spikes(drawn, jax.random.fold_in(rng, 3), *heavy), -reach, reach).astype(dtype)


def setup_inputs(seed: int = 0) -> dict:
    streams_of = jax.random.split(jax.random.key(seed), 8)
    activations = bell_draw(streams_of[0], (TOK, D), 1.0, 6.0, ((1, 8),))
    cotangent = bell_draw(streams_of[1], (TOK, D), 1.0, 6.0, ((1, 8),))
    up_weight = bell_draw(streams_of[2], (LAYERS, D, FF), D ** -0.5, 0.0625, ((1, 8), (2, 64)))
    down_weight = bell_draw(streams_of[3], (LAYERS, FF, D), FF ** -0.5, 0.03125, ((1, 64), (2, 8)))
    width_proj = bell_draw(streams_of[4], (K, D), D ** -0.5, 0.0625, ((1, 8),))
    hidden_proj = bell_draw(streams_of[5], (K, FF), (FF // 4) ** -0.5, 0.0625, ((1, 64),))
    queries = bell_draw_with(streams_of[6], (NQ, MATS * K * K), (MATS * K * K * LEN // 8) ** -0.5, 0.03125, ((0, 8), (1, 64)), (1, 0, 64, 4.0))
    return {"activations": activations, "cotangent": cotangent, "up_weight": up_weight, "down_weight": down_weight, "width_proj": width_proj, "hidden_proj": hidden_proj, "queries": queries}


def silu_slope(values):
    sigma_val = jax.nn.sigmoid(values)
    return sigma_val * (1.0 + values * (1.0 - sigma_val))


def tensor_sum(operand, factor):
    block_width = operand.shape[1] // N_TENSOR
    running = jnp.zeros((operand.shape[0], factor.shape[1]), jnp.float32)
    for block in range(N_TENSOR):
        partial_value = jnp.dot(operand[:, block * block_width:(block + 1) * block_width],
                          factor[block * block_width:(block + 1) * block_width],
                          preferred_element_type=jnp.float32)
        running = running + lax.optimization_barrier(partial_value.astype(jnp.bfloat16)).astype(jnp.float32)
    return running


def project(operand, factor):
    return lax.dot_general(operand, factor, (((1,), (1,)), ((), ())), preferred_element_type=jnp.float32)


def outer_sums(inputs, outputs):
    first = inputs.reshape(EX, LEN, K)
    second = outputs.reshape(EX, LEN, K)
    return jnp.einsum("elk,elj->ekj", first, second, precision=lax.Precision.HIGHEST).reshape(EX, K * K)


def reference(activations, cotangent, up_weight, down_weight, width_proj, hidden_proj, queries):
    width_t = width_proj.T
    pre_one = tensor_sum(activations, up_weight[0])
    left_zero = tensor_sum(activations, width_t)
    act_one = jax.nn.silu(pre_one).astype(jnp.bfloat16)
    out_one = jnp.dot(act_one, down_weight[0], preferred_element_type=jnp.float32)
    left_one = project(act_one, hidden_proj)
    resid_two = (activations.astype(jnp.float32) + out_one).astype(jnp.bfloat16)
    pre_two = tensor_sum(resid_two, up_weight[1])
    left_two = tensor_sum(resid_two, width_t)
    act_two = jax.nn.silu(pre_two).astype(jnp.bfloat16)
    left_three = project(act_two, hidden_proj)
    back_two = tensor_sum(cotangent, down_weight[1].T)
    right_three = tensor_sum(cotangent, width_t)
    delta_two = (back_two * silu_slope(pre_two)).astype(jnp.bfloat16)
    back_sum = project(delta_two, up_weight[1])
    right_two = project(delta_two, hidden_proj)
    grad_one = (cotangent.astype(jnp.float32) + back_sum).astype(jnp.bfloat16)
    back_one = tensor_sum(grad_one, down_weight[0].T)
    right_one = tensor_sum(grad_one, width_t)
    delta_one = (back_one * silu_slope(pre_one)).astype(jnp.bfloat16)
    right_zero = project(delta_one, hidden_proj)
    input_grad = (grad_one.astype(jnp.float32) + project(delta_one, up_weight[0])).astype(jnp.bfloat16)
    grads = jnp.concatenate([outer_sums(left_zero, right_zero), outer_sums(left_one, right_one),
                             outer_sums(left_two, right_two), outer_sums(left_three, right_three)], axis=1)
    scores = jnp.dot(grads, queries.astype(jnp.float32).T, precision=lax.Precision.HIGHEST)
    return scores, input_grad
```

```python
import functools

import jax
import jax.numpy as jnp
from jax import lax
from jax.experimental import pallas as pl
from jax.experimental.pallas import tpu as pltpu
from jax.sharding import PartitionSpec as P

MESH = pl.DeviceIdType.MESH
F32, BF16 = jnp.float32, jnp.bfloat16
EX = 2
M = 128
T = 8
NZ = 16
B = M // T
D = 1024
H = 448
K = 64
W = H + K
C_WIDTH = W + 2 * K


def silu_slope(values):
    sigma = jax.nn.sigmoid(values)
    return sigma * (1.0 + values * (1.0 - sigma))


def dot(a, b):
    return jnp.dot(a, b, preferred_element_type=F32)


def against(a, b):
    return lax.dot_general(a, b, (((1,), (1,)), ((), ())), preferred_element_type=F32)


def take(ref, sem):
    pltpu.make_async_copy(ref, ref, sem).wait()


def kernel(
    act_hbm, cot_hbm, up_hbm, down_hbm, width_hbm, hidden_hbm, query_hbm,
    score_ref, grad_ref,
    act, cot, up0, up1, dn0, dn1, hid, qry, load_sem,
    t_part, t_got, t_all, c_all, t_send, t_recv, pre_one,
    s_part, s_core, s_ysend, s_yrecv, s_z, s_zrecv, s_all, s_send, s_recv, full32, half32,
    f_turn, f_z, f_zrecv,
    g_part, g_core, g_sum, g_yrecv, g_z, g_zrecv, g_send, g_recv,
    p_part, p_recv, p_zrecv,
    left, right,
):
    s = lax.axis_index("section")
    t = lax.axis_index("tensor")
    z, y, c = s // 4, (s // 2) % 2, s % 2

    def section(zz, yy, cc):
        return {"section": zz * 4 + yy * 2 + cc}

    core_peer = section(z, y, 1 - c)
    y_peer = section(z, 1 - y, c)

    def z_at(i):
        far = (i + 1) // 2
        return lax.rem(z + 8 + jnp.where(i % 2 == 0, far, -far), NZ)

    def z_peer(i):
        return section(z_at(i), y, c)

    def t_at(i):
        return t ^ (i + 1)

    def t_peer(i):
        return {"tensor": t_at(i)}

    loads = {}

    def load(name, pairs, slot):
        copies = [pltpu.make_async_copy(a, b, load_sem.at[slot + n]) for n, (a, b) in enumerate(pairs)]
        for one in copies:
            one.start()
        loads[name] = copies

    def ready(name):
        for one in loads.pop(name, ()):
            one.wait()

    load("act", [(act_hbm, act)], 0)
    load("up0", [(up_hbm.at[0], up0), (width_hbm, dn0.at[pl.ds(H, K)])], 1)
    load("dn1", [(cot_hbm, cot), (down_hbm.at[1], dn1.at[pl.ds(0, H)]), (width_hbm, dn1.at[pl.ds(H, K)])], 3)
    load("dn0", [(down_hbm.at[0], dn0.at[pl.ds(0, H)]), (hidden_hbm, hid)], 6)
    load("up1", [(up_hbm.at[1], up1)], 8)
    load("qry", [(query_hbm, qry)], 9)

    barrier = pltpu.get_barrier_semaphore()

    def greet(device):
        pl.semaphore_signal(barrier, inc=1, device_id=device, device_id_type=MESH)

    def greet_many(n, peer):
        def one(i, carry):
            greet(peer(i))
            return carry
        lax.fori_loop(0, n, one, 0)

    greet_many(NZ - 1, z_peer)
    greet_many(T - 1, t_peer)
    greet(y_peer)
    greet(core_peer)

    sent = []

    def push(src, dst, peer, send_sem, recv_sem):
        pltpu.make_async_remote_copy(
            src_ref=src, dst_ref=dst, send_sem=send_sem, recv_sem=recv_sem,
            device_id=peer, device_id_type=MESH,
        ).start()

    def fan(n, peer, src, dst, send_sem, recv_sem, whole):
        def one(i, carry):
            push(src(i), dst(i), peer(i), send_sem, recv_sem)
            return carry
        lax.fori_loop(0, n, one, 0)
        sent.append((whole, send_sem))

    def push_one(src, dst, peer, send_sem, recv_sem):
        push(src, dst, peer, send_sem, recv_sem)
        sent.append((dst, send_sem))

    rows_of = lambda i, n: pl.ds(pl.multiple_of(i * n, n), n)

    def t_scatter(x, h):
        fan(
            T - 1, t_peer,
            lambda i: t_part.at[x, h, rows_of(t_at(i), B)],
            lambda i: t_got.at[x, h, i],
            t_send.at[0, x, h], t_recv.at[0, x, h], t_got.at[x, h],
        )

    def t_total(x, h):
        take(t_got.at[x, h], t_recv.at[0, x, h])
        total = t_part[x, h, rows_of(t, B), :].astype(F32)
        for i in range(T - 1):
            total += t_got[x, h, i].astype(F32)
        return total

    def t_gather(x, h, buf):
        mine = buf.at[h, rows_of(t, B)]
        others = buf.at[h, pl.ds(0, B * (T - 1))]
        fan(T - 1, t_peer, lambda i: mine, lambda i: mine, t_send.at[1, x, h], t_recv.at[1, x, h], others)
        return others

    def s_reduce(p, h, value):
        full32[h] = value
        s_part[p, h] = value.astype(BF16)
        push_one(s_part.at[p, h, rows_of(1 - c, M // 2)], s_core.at[p, h], core_peer, s_send.at[0, p, h], s_recv.at[0, p, h])
        yield
        take(s_core.at[p, h], s_recv.at[0, p, h])

        def quarter(yy):
            mine = full32[h, rows_of(2 * c + yy, M // 4), :]
            return mine + s_core[p, h, rows_of(yy, M // 4), :].astype(F32)

        s_ysend[p, h] = quarter(1 - y).astype(BF16)
        push_one(s_ysend.at[p, h], s_yrecv.at[p, h], y_peer, s_send.at[1, p, h], s_recv.at[1, p, h])
        half32[h] = quarter(y)
        yield
        take(s_yrecv.at[p, h], s_recv.at[1, p, h])
        return half32[h] + s_yrecv[p, h].astype(F32)

    def s_scatter(p, h, value):
        for ig in range(2):
            for j in range(8):
                s_z[p, h, ig * 8 + j] = value[B * ig:B * ig + B, 128 * j:128 * j + 128].astype(BF16)
        fan(
            NZ - 1, z_peer, lambda i: s_z.at[p, h, z_at(i)], lambda i: s_zrecv.at[p, h, i],
            s_send.at[2, p, h], s_recv.at[2, p, h], s_zrecv.at[p, h],
        )
        yield
        take(s_zrecv.at[p, h], s_recv.at[2, p, h])
        total = s_z[p, h, z].astype(F32)
        for i in range(NZ - 1):
            total += s_zrecv[p, h, i].astype(F32)
        return total

    tile_row = pl.multiple_of(c * (M // 2) + y * (M // 4) + (z // 8) * B, B)
    tile_col = pl.multiple_of((z % 8) * 128, 128)

    def s_gather(p, h, tile):
        spot = s_all.at[p, h, pl.ds(tile_row, B), pl.ds(tile_col, 128)]
        s_all[p, h, pl.ds(tile_row, B), pl.ds(tile_col, 128)] = tile
        fan(NZ - 1, z_peer, lambda i: spot, lambda i: spot, s_send.at[3, p, h], s_recv.at[3, p, h], s_zrecv.at[p, h])
        yield
        take(s_zrecv.at[p, h], s_recv.at[3, p, h])
        quarter = s_all.at[p, h, rows_of(2 * c + y, M // 4)]
        push_one(quarter, quarter, y_peer, s_send.at[4, p, h], s_recv.at[4, p, h])
        yield
        take(quarter, s_recv.at[4, p, h])
        half = s_all.at[p, h, rows_of(c, M // 2)]
        push_one(half, half, core_peer, s_send.at[5, p, h], s_recv.at[5, p, h])
        yield
        take(half, s_recv.at[5, p, h])

    def tile_of(ref, h):
        return ref[pl.ds(pl.multiple_of(h * M + tile_row, B), B), pl.ds(tile_col, 128)].astype(F32)

    def spread(h):
        q = lax.broadcasted_iota(jnp.int32, (2 * K, K), 0)
        a = lax.broadcasted_iota(jnp.int32, (2 * K, K), 1)
        pick = (a == (q // 8) * 4 + q % 4) & ((q // 4) % 2 == h)
        return jnp.where(pick, 1.0, 0.0).astype(BF16)

    def products(m):
        total = None
        for h in range(EX):
            turned = against(spread(h), left[m, h]).astype(BF16)
            part = dot(turned, right[m, h])
            total = part if total is None else total + part
        for i in range(16):
            g_part[i % 2, (i // 2) % 2, 4 * m + i // 4, :, pl.ds(0, K)] = total[8 * i:8 * i + 8]

    def stream(h):
        rows = slice(h * M, h * M + M)
        lanes = lax.broadcasted_iota(jnp.int32, (B, W), 1)
        if h == 0:
            ready("act")
            ready("up0")
        t_part[0, h, :, pl.ds(0, H)] = dot(act[rows], up0[...]).astype(BF16)
        t_part[0, h, :, pl.ds(H, K)] = against(act[rows], dn0[pl.ds(H, K), :]).astype(BF16)
        if h == 0:
            pl.semaphore_wait(barrier, NZ - 1 + T - 1 + 2)
        t_scatter(0, h)
        yield
        if h == 0:
            ready("dn1")
        t_part[1, h] = against(cot[rows], dn1[...]).astype(BF16)
        t_scatter(1, h)
        total = t_total(0, h)
        pre_one[h] = total
        t_all[0, h, rows_of(t, B), :] = jnp.where(lanes < H, jax.nn.silu(total), total).astype(BF16)
        others = t_gather(0, h, t_all.at[0])
        yield
        if h == 0:
            ready("dn0")
        take(others, t_recv.at[1, 0, h])
        act_one = t_all[0, h, :, pl.ds(0, H)]
        going = s_reduce(0, h, dot(act_one, dn0[pl.ds(0, H), :]))
        next(going)
        left[0, h] = t_all[0, h, :, pl.ds(H, K)]
        left[1, h] = against(act_one, hid[...]).astype(BF16)
        yield
        value = yield from going
        value = yield from s_scatter(0, h, value)
        yield from s_gather(0, h, (tile_of(act, h) + value).astype(BF16))
        if h == 0:
            ready("up1")
        resid = s_all[0, h]
        t_part[2, h, :, pl.ds(0, H)] = dot(resid, up1[...]).astype(BF16)
        t_part[2, h, :, pl.ds(H, K)] = against(resid, dn0[pl.ds(H, K), :]).astype(BF16)
        t_scatter(2, h)
        back = t_total(1, h)
        yield
        total = t_total(2, h)
        act_two = jax.nn.silu(total[:, :H]).astype(BF16)
        own = rows_of(t, B)
        c_all[h, own, pl.ds(0, W)] = jnp.where(lanes < H, back * silu_slope(total), total).astype(BF16)
        c_all[h, own, pl.ds(W, K)] = against(act_two, hid[...]).astype(BF16)
        c_all[h, own, pl.ds(W + K, K)] = back[:, H:].astype(BF16)
        others = t_gather(2, h, c_all)
        yield
        take(others, t_recv.at[1, 2, h])
        delta_two = c_all[h, :, pl.ds(0, H)]
        going = s_reduce(1, h, against(delta_two, up1[...]))
        next(going)
        left[2, h] = c_all[h, :, pl.ds(H, K)]
        left[3, h] = c_all[h, :, pl.ds(W, K)]
        right[3, h] = c_all[h, :, pl.ds(W + K, K)]
        right[2, h] = against(delta_two, hid[...]).astype(BF16)
        yield
        value = yield from going
        value = yield from s_scatter(1, h, value)
        yield from s_gather(1, h, (tile_of(cot, h) + value).astype(BF16))
        t_part[3, h] = against(s_all[1, h], dn0[...]).astype(BF16)
        t_scatter(3, h)
        if h == 1:
            products(2)
            products(3)
        yield
        total = t_total(3, h)
        t_all[1, h, rows_of(t, B), :] = jnp.where(lanes < H, total * silu_slope(pre_one[h]), total).astype(BF16)
        others = t_gather(3, h, t_all.at[1])
        yield
        take(others, t_recv.at[1, 3, h])
        delta_one = t_all[1, h, :, pl.ds(0, H)]
        to = lax.broadcasted_iota(jnp.int32, (M, M), 0)
        came = lax.broadcasted_iota(jnp.int32, (M, M), 1)
        source = ((to // 4) % 8) * 16 + ((to // 32) % 2) * 8 + (to // 64) * 4 + to % 4
        turn = jnp.where(came == source, 1.0, 0.0).astype(BF16)
        turned = dot(turn, delta_one).astype(BF16)
        going = s_reduce(2, h, against(turned, up0[...]))
        next(going)
        right[1, h] = t_all[1, h, :, pl.ds(H, K)]
        right[0, h] = against(delta_one, hid[...]).astype(BF16)
        yield
        if h == 1:
            going_on = next(going, None)
            products(0)
            products(1)
            push_one(g_part.at[1 - c], g_core, core_peer, g_send.at[0], g_recv.at[0])
            yield
        value = yield from going
        half32[h] = value
        for zz in range(8):
            for j in range(8):
                f_turn[pl.ds(4 * j, 4), :] = half32[h, pl.ds(4 * zz, 4), pl.ds(128 * j, 128)]
            f_z[8 * h + zz] = f_turn[...].astype(BF16)

    streams = [stream(h) for h in range(EX)]
    g_part[...] = jnp.zeros_like(g_part)
    while streams:
        for one in list(streams):
            try:
                next(one)
            except StopIteration:
                streams.remove(one)

    fan(NZ - 1, z_peer, lambda i: f_z.at[z_at(i)], lambda i: f_zrecv.at[i], g_send.at[6], g_recv.at[6], f_zrecv)

    take(g_core, g_recv.at[0])
    g_sum[...] = g_part[c] + g_core[...]
    push_one(g_sum.at[1 - y], g_yrecv, y_peer, g_send.at[1], g_recv.at[1])
    take(g_yrecv, g_recv.at[1])
    g_z[...] = g_sum[y] + g_yrecv[...]
    fan(NZ - 1, z_peer, lambda i: g_z.at[z_at(i)], lambda i: g_zrecv.at[i], g_send.at[2], g_recv.at[2], g_zrecv)
    take(g_zrecv, g_recv.at[2])
    slab = g_z[z]
    for i in range(NZ - 1):
        slab += g_zrecv[i]

    ready("qry")
    one = slab[:, :K]
    wide = jnp.concatenate([one, one, one, one], axis=1)
    at_row = lax.broadcasted_iota(jnp.int32, (8, 4 * K), 0) % 4
    at_lane = lax.broadcasted_iota(jnp.int32, (8, 4 * K), 1) // K
    wide = jnp.where(at_row == at_lane, wide, 0.0)
    high = wide.astype(BF16)
    low = (wide - high.astype(F32)).astype(BF16)
    part = against(high, qry[...]) + against(low, qry[...])
    p_part[...] = jnp.zeros_like(p_part)
    p_part[0, :, pl.ds(0, K)] = part
    push_one(p_part.at[0], p_recv.at[0], core_peer, g_send.at[3], g_recv.at[3])
    take(p_recv.at[0], g_recv.at[3])
    p_part[1] = p_part[0] + p_recv[0]
    push_one(p_part.at[1], p_recv.at[1], y_peer, g_send.at[4], g_recv.at[4])
    take(p_recv.at[1], g_recv.at[4])
    p_part[2] = p_part[1] + p_recv[1]
    fan(NZ - 1, z_peer, lambda i: p_part.at[2], lambda i: p_zrecv.at[i], g_send.at[5], g_recv.at[5], p_zrecv)

    take(f_zrecv, g_recv.at[6])
    total = f_z[z].astype(F32)
    for i in range(NZ - 1):
        total += f_zrecv[i].astype(F32)
    group = s_all[1, z // 8, rows_of(z % 8, 16), :].astype(F32)
    place = 2 * y + c
    own = group[0:4]
    for n in range(1, 4):
        own = jnp.where(place == n, group[4 * n:4 * n + 4], own)
    for j in range(8):
        grad_ref[:, pl.ds(128 * j, 128)] = (own[:, 128 * j:128 * j + 128] + total[4 * j:4 * j + 4]).astype(BF16)

    take(p_zrecv, g_recv.at[5])
    total = p_part[2]
    for i in range(NZ - 1):
        total += p_zrecv[i]
    score_ref[pl.ds(0, 1), :] = jnp.sum(total[0:4, :K], axis=0, keepdims=True)
    score_ref[pl.ds(1, 1), :] = jnp.sum(total[4:8, :K], axis=0, keepdims=True)

    for whole, sem in sent:
        take(whole, sem)


def on_device(*operands):
    dma, vmem = pltpu.SemaphoreType.DMA, pltpu.VMEM
    scratch = [
        vmem((EX * M, D), BF16), vmem((EX * M, D), BF16), vmem((D, H), BF16), vmem((D, H), BF16),
        vmem((W, D), BF16), vmem((W, D), BF16), vmem((K, H), BF16), vmem((K, 4 * K), BF16), dma((10,)),
        vmem((4, EX, M, W), BF16), vmem((4, EX, T - 1, B, W), BF16), vmem((2, EX, M, W), BF16), vmem((EX, M, C_WIDTH), BF16),
        dma((2, 4, EX)), dma((2, 4, EX)), vmem((EX, B, W), F32),
        vmem((3, EX, M, D), BF16), vmem((3, EX, M // 2, D), BF16), vmem((3, EX, M // 4, D), BF16), vmem((3, EX, M // 4, D), BF16),
        vmem((2, EX, NZ, B, 128), BF16), vmem((2, EX, NZ - 1, B, 128), BF16), vmem((2, EX, M, D), BF16),
        dma((6, 3, EX)), dma((6, 3, EX)), vmem((EX, M, D), F32), vmem((EX, M // 4, D), F32),
        vmem((32, 128), F32), vmem((NZ, 32, 128), BF16), vmem((NZ - 1, 32, 128), BF16),
        vmem((2, 2, NZ, 8, 128), F32), vmem((2, NZ, 8, 128), F32), vmem((2, NZ, 8, 128), F32), vmem((NZ, 8, 128), F32),
        vmem((NZ, 8, 128), F32), vmem((NZ - 1, 8, 128), F32), dma((7,)), dma((7,)),
        vmem((3, 8, 128), F32), vmem((2, 8, 128), F32), vmem((NZ - 1, 8, 128), F32),
        vmem((4, EX, M, K), BF16), vmem((4, EX, M, K), BF16),
    ]
    return pl.pallas_call(
        kernel,
        name="window",
        out_shape=(jax.ShapeDtypeStruct((EX, K), F32), jax.ShapeDtypeStruct((4, D), BF16)),
        in_specs=[pl.BlockSpec(memory_space=pl.ANY)] * 7,
        out_specs=(pl.BlockSpec(memory_space=pltpu.VMEM), pl.BlockSpec(memory_space=pltpu.VMEM)),
        scratch_shapes=scratch,
        compiler_params=pltpu.CompilerParams(collective_id=0, has_side_effects=True, vmem_limit_bytes=48 << 20),
        cost_estimate=pl.CostEstimate(flops=2 * 10**9, bytes_accessed=5 * 10**6, transcendentals=0),
    )(*operands)


def solution(mesh):
    placed = (
        P(None, "tensor"),
        P(None, "tensor"),
        P(None, "tensor", "section"),
        P(None, "section", "tensor"),
        P(None, "tensor"),
        P(None, "section"),
        P("tensor", "section"),
    )
    return jax.shard_map(
        on_device,
        mesh=mesh,
        in_specs=placed,
        out_specs=(P(None, "tensor"), P("section", "tensor")),
        check_vma=False,
    )
```

```python
import functools

import jax
import jax.numpy as jnp
from jax import lax
from jax.experimental import pallas as pl
from jax.experimental.pallas import tpu as pltpu
from jax.sharding import PartitionSpec as P

MESH = pl.DeviceIdType.MESH
F32, BF16 = jnp.float32, jnp.bfloat16
EX = 2
M = 128
T = 8
NZ = 16
B = M // T
D = 1024
H = 448
K = 64
W = H + K
C_WIDTH = W + 2 * K


def silu_slope(values):
    sigma = jax.nn.sigmoid(values)
    return sigma * (1.0 + values * (1.0 - sigma))


def dot(a, b):
    return jnp.dot(a, b, preferred_element_type=F32)


def against(a, b):
    return lax.dot_general(a, b, (((1,), (1,)), ((), ())), preferred_element_type=F32)


def take(ref, sem):
    pltpu.make_async_copy(ref, ref, sem).wait()


def kernel(
    act_hbm, cot_hbm, up_hbm, down_hbm, width_hbm, hidden_hbm, query_hbm,
    score_ref, grad_ref,
    act, cot, up0, up1, dn0, dn1, hid, q_all, load_sem, q_send, q_recv,
    t_part, t_got, t_all, c_all, t_send, t_recv, pre_one,
    s_part, s_core, s_ysend, s_yrecv, s_z, s_zrecv, s_all, s_send, s_recv, full32, half32,
    f_turn, f_z, f_zrecv,
    f_send, f_recv, g_part, g_core, g_sum, g_yrecv, g_send, g_recv,
    p_part, p_recv, p_zrecv, p_send, p_recv_sem,
    left, right,
):
    s = lax.axis_index("section")
    t = lax.axis_index("tensor")
    z, y, c = s // 4, (s // 2) % 2, s % 2

    def section(zz, yy, cc):
        return {"section": zz * 4 + yy * 2 + cc}

    core_peer = section(z, y, 1 - c)
    y_peer = section(z, 1 - y, c)

    def z_at(i):
        far = (i + 1) // 2
        return lax.rem(z + 8 + jnp.where(i % 2 == 0, far, -far), NZ)

    def z_peer(i):
        return section(z_at(i), y, c)

    def t_at(i):
        return t ^ (i + 1)

    def t_peer(i):
        return {"tensor": t_at(i)}

    loads = {}

    def load(name, pairs, slot):
        copies = [pltpu.make_async_copy(a, b, load_sem.at[slot + n]) for n, (a, b) in enumerate(pairs)]
        for one in copies:
            one.start()
        loads[name] = copies

    def ready(name):
        for one in loads.pop(name, ()):
            one.wait()

    def weight(name, ref, buf, slot):
        load(name, [(ref, buf.at[pl.ds(0, H)]), (width_hbm, buf.at[pl.ds(H, K)])], slot)

    load("act", [(act_hbm, act)], 0)
    weight("up0", up_hbm.at[0], up0, 1)
    load("cot", [(cot_hbm, cot)], 3)
    weight("dn1", down_hbm.at[1], dn1, 4)
    weight("dn0", down_hbm.at[0], dn0, 6)
    load("hid", [(hidden_hbm, hid)], 8)
    load("qry", [(query_hbm, q_all.at[z])], 9)
    weight("up1", up_hbm.at[1], up1, 10)

    barrier = pltpu.get_barrier_semaphore()

    def greet(device):
        pl.semaphore_signal(barrier, inc=1, device_id=device, device_id_type=MESH)

    def greet_many(n, peer):
        def one(i, carry):
            greet(peer(i))
            return carry
        lax.fori_loop(0, n, one, 0)

    greet_many(NZ - 1, z_peer)
    greet_many(T - 1, t_peer)
    greet(y_peer)
    greet(core_peer)

    sent = []

    def push(src, dst, peer, send_sem, recv_sem):
        pltpu.make_async_remote_copy(
            src_ref=src, dst_ref=dst, send_sem=send_sem, recv_sem=recv_sem,
            device_id=peer, device_id_type=MESH,
        ).start()

    def fan(n, peer, src, dst, send_sem, recv_sem, whole):
        def one(i, carry):
            push(src(i), dst(i), peer(i), send_sem, recv_sem)
            return carry
        lax.fori_loop(0, n, one, 0)
        sent.append((whole, send_sem))

    def push_one(src, dst, peer, send_sem, recv_sem):
        push(src, dst, peer, send_sem, recv_sem)
        sent.append((dst, send_sem))

    steps = []

    def q_step():
        k = len(steps)
        if k == 0:
            ready("qry")
        for way in range(2):
            if 0 < k and (k < NZ // 2 or way == 0):
                take(q_all.at[0], q_recv.at[way, k - 1])
        steps.append(k)
        if k == NZ // 2:
            return
        for way, sign in enumerate((1, -1)):
            if k < NZ // 2 - 1 or way == 0:
                block = q_all.at[lax.rem(z - sign * k + NZ, NZ)]
                push_one(block, block, section(lax.rem(z + sign + NZ, NZ), y, c), q_send.at[way, k], q_recv.at[way, k])

    rows_of = lambda i, n: pl.ds(pl.multiple_of(i * n, n), n)

    def t_scatter(x, h):
        fan(
            T - 1, t_peer,
            lambda i: t_part.at[x, h, rows_of(t_at(i), B)],
            lambda i: t_got.at[x, h, i],
            t_send.at[0, x, h], t_recv.at[0, x, h], t_got.at[x, h],
        )

    def t_total(x, h):
        take(t_got.at[x, h], t_recv.at[0, x, h])
        total = t_part[x, h, rows_of(t, B), :].astype(F32)
        for i in range(T - 1):
            total += t_got[x, h, i].astype(F32)
        return total

    def t_gather(x, h, buf):
        mine = buf.at[h, rows_of(t, B)]
        others = buf.at[h, pl.ds(0, B * (T - 1))]
        fan(T - 1, t_peer, lambda i: mine, lambda i: mine, t_send.at[1, x, h], t_recv.at[1, x, h], others)
        return others

    def s_reduce(p, h, value):
        full32[h] = value
        s_part[p, h] = value.astype(BF16)
        push_one(s_part.at[p, h, rows_of(1 - c, M // 2)], s_core.at[p, h], core_peer, s_send.at[0, p, h], s_recv.at[0, p, h])
        yield
        take(s_core.at[p, h], s_recv.at[0, p, h])

        def quarter(yy):
            mine = full32[h, rows_of(2 * c + yy, M // 4), :]
            return mine + s_core[p, h, rows_of(yy, M // 4), :].astype(F32)

        s_ysend[p, h] = quarter(1 - y).astype(BF16)
        push_one(s_ysend.at[p, h], s_yrecv.at[p, h], y_peer, s_send.at[1, p, h], s_recv.at[1, p, h])
        half32[h] = quarter(y)
        yield
        take(s_yrecv.at[p, h], s_recv.at[1, p, h])
        return half32[h] + s_yrecv[p, h].astype(F32)

    def s_scatter(p, h, value):
        for ig in range(2):
            for j in range(8):
                s_z[p, h, ig * 8 + j] = value[B * ig:B * ig + B, 128 * j:128 * j + 128].astype(BF16)
        fan(
            NZ - 1, z_peer, lambda i: s_z.at[p, h, z_at(i)], lambda i: s_zrecv.at[p, h, i],
            s_send.at[2, p, h], s_recv.at[2, p, h], s_zrecv.at[p, h],
        )
        yield
        take(s_zrecv.at[p, h], s_recv.at[2, p, h])
        total = s_z[p, h, z].astype(F32)
        for i in range(NZ - 1):
            total += s_zrecv[p, h, i].astype(F32)
        return total

    tile_row = pl.multiple_of(c * (M // 2) + y * (M // 4) + (z // 8) * B, B)
    tile_col = pl.multiple_of((z % 8) * 128, 128)

    def s_gather(p, h, tile):
        spot = s_all.at[p, h, pl.ds(tile_row, B), pl.ds(tile_col, 128)]
        s_all[p, h, pl.ds(tile_row, B), pl.ds(tile_col, 128)] = tile
        fan(NZ - 1, z_peer, lambda i: spot, lambda i: spot, s_send.at[3, p, h], s_recv.at[3, p, h], s_zrecv.at[p, h])
        yield
        take(s_zrecv.at[p, h], s_recv.at[3, p, h])
        quarter = s_all.at[p, h, rows_of(2 * c + y, M // 4)]
        push_one(quarter, quarter, y_peer, s_send.at[4, p, h], s_recv.at[4, p, h])
        yield
        take(quarter, s_recv.at[4, p, h])
        half = s_all.at[p, h, rows_of(c, M // 2)]
        push_one(half, half, core_peer, s_send.at[5, p, h], s_recv.at[5, p, h])
        yield
        take(half, s_recv.at[5, p, h])

    def tile_of(ref, h):
        return ref[pl.ds(pl.multiple_of(h * M + tile_row, B), B), pl.ds(tile_col, 128)].astype(F32)

    def spread(h):
        q = lax.broadcasted_iota(jnp.int32, (2 * K, K), 0)
        a = lax.broadcasted_iota(jnp.int32, (2 * K, K), 1)
        pick = (a == (q // 8) * 4 + q % 4) & ((q // 4) % 2 == h)
        return jnp.where(pick, 1.0, 0.0).astype(BF16)

    def products(m):
        total = None
        for h in range(EX):
            turned = against(spread(h), left[m, h]).astype(BF16)
            part = dot(turned, right[m, h])
            total = part if total is None else total + part
        for i in range(16):
            g_part[m // 2, i % 2, (i // 2) % 2, 4 * (m % 2) + i // 4, :, pl.ds(0, K)] = total[8 * i:8 * i + 8]

    def g_swap(u):
        products(2 * u)
        products(2 * u + 1)
        push_one(g_part.at[u, 1 - c], g_core.at[u], core_peer, g_send.at[0, u], g_recv.at[0, u])

    def g_cross(u):
        take(g_core.at[u], g_recv.at[0, u])
        g_sum[u] = g_part[u, c] + g_core[u]
        push_one(g_sum.at[u, 1 - y], g_yrecv.at[u], y_peer, g_send.at[1, u], g_recv.at[1, u])

    at_row = lax.broadcasted_iota(jnp.int32, (8, 4 * K), 0) % 4
    at_lane = lax.broadcasted_iota(jnp.int32, (8, 4 * K), 1) // K

    def g_score(u):
        take(g_yrecv.at[u], g_recv.at[1, u])
        total = jnp.zeros((16, K), F32)
        for i in range(8):
            one = (g_sum[u, y, i] + g_yrecv[u, i])[:, :K]
            wide = jnp.where(at_row == at_lane, jnp.concatenate([one, one, one, one], axis=1), 0.0)
            high = wide.astype(BF16).astype(F32)
            both = jnp.concatenate([high, wide - high], axis=0).astype(BF16)
            total += against(both, q_all[8 * u + i])
        return total

    def stream(h):
        rows = slice(h * M, h * M + M)
        lanes = lax.broadcasted_iota(jnp.int32, (B, W), 1)
        if h == 0:
            ready("act")
            ready("up0")
        t_part[0, h] = against(act[rows], up0[...]).astype(BF16)
        if h == 0:
            pl.semaphore_wait(barrier, NZ - 1 + T - 1 + 2)
        t_scatter(0, h)
        yield
        if h == 0:
            ready("cot")
            ready("dn1")
        t_part[1, h] = against(cot[rows], dn1[...]).astype(BF16)
        t_scatter(1, h)
        total = t_total(0, h)
        pre_one[h] = total
        t_all[0, h, rows_of(t, B), :] = jnp.where(lanes < H, jax.nn.silu(total), total).astype(BF16)
        others = t_gather(0, h, t_all.at[0])
        yield
        if h == 0:
            ready("dn0")
            ready("hid")
        take(others, t_recv.at[1, 0, h])
        act_one = t_all[0, h, :, pl.ds(0, H)]
        going = s_reduce(0, h, dot(act_one, dn0[pl.ds(0, H), :]))
        next(going)
        left[0, h] = t_all[0, h, :, pl.ds(H, K)]
        left[1, h] = against(act_one, hid[...]).astype(BF16)
        yield
        value = yield from going
        value = yield from s_scatter(0, h, value)
        yield from s_gather(0, h, (tile_of(act, h) + value).astype(BF16))
        if h == 0:
            ready("up1")
        resid = s_all[0, h]
        t_part[2, h] = against(resid, up1[...]).astype(BF16)
        t_scatter(2, h)
        back = t_total(1, h)
        yield
        total = t_total(2, h)
        act_two = jax.nn.silu(total[:, :H]).astype(BF16)
        own = rows_of(t, B)
        c_all[h, own, pl.ds(0, W)] = jnp.where(lanes < H, back * silu_slope(total), total).astype(BF16)
        c_all[h, own, pl.ds(W, K)] = against(act_two, hid[...]).astype(BF16)
        c_all[h, own, pl.ds(W + K, K)] = back[:, H:].astype(BF16)
        others = t_gather(2, h, c_all)
        yield
        take(others, t_recv.at[1, 2, h])
        delta_two = c_all[h, :, pl.ds(0, H)]
        going = s_reduce(1, h, dot(delta_two, up1[pl.ds(0, H), :]))
        next(going)
        left[2, h] = c_all[h, :, pl.ds(H, K)]
        left[3, h] = c_all[h, :, pl.ds(W, K)]
        right[3, h] = c_all[h, :, pl.ds(W + K, K)]
        right[2, h] = against(delta_two, hid[...]).astype(BF16)
        yield
        value = yield from going
        value = yield from s_scatter(1, h, value)
        yield from s_gather(1, h, (tile_of(cot, h) + value).astype(BF16))
        t_part[3, h] = against(s_all[1, h], dn0[...]).astype(BF16)
        t_scatter(3, h)
        if h == 1:
            g_swap(1)
        yield
        total = t_total(3, h)
        t_all[1, h, rows_of(t, B), :] = jnp.where(lanes < H, total * silu_slope(pre_one[h]), total).astype(BF16)
        others = t_gather(3, h, t_all.at[1])
        if h == 1:
            g_cross(1)
        yield
        take(others, t_recv.at[1, 3, h])
        delta_one = t_all[1, h, :, pl.ds(0, H)]
        to = lax.broadcasted_iota(jnp.int32, (M, M), 0)
        came = lax.broadcasted_iota(jnp.int32, (M, M), 1)
        source = ((to // 4) % 8) * 16 + ((to // 32) % 2) * 8 + (to // 64) * 4 + to % 4
        turn = jnp.where(came == source, 1.0, 0.0).astype(BF16)
        turned = dot(turn, delta_one).astype(BF16)
        going = s_reduce(2, h, dot(turned, up0[pl.ds(0, H), :]))
        next(going)
        right[1, h] = t_all[1, h, :, pl.ds(H, K)]
        right[0, h] = against(delta_one, hid[...]).astype(BF16)
        yield
        if h == 1:
            next(going)
            g_swap(0)
            yield
        value = yield from going
        half32[h] = value
        for zz in range(8):
            for j in range(8):
                f_turn[pl.ds(4 * j, 4), :] = half32[h, pl.ds(4 * zz, 4), pl.ds(128 * j, 128)]
            f_z[8 * h + zz] = f_turn[...].astype(BF16)

    streams = [stream(h) for h in range(EX)]
    g_part[...] = jnp.zeros_like(g_part)
    turns = 0
    while streams:
        for one in list(streams):
            try:
                next(one)
            except StopIteration:
                streams.remove(one)
        if turns % 2 == 0 and turns // 2 <= NZ // 2:
            q_step()
        turns += 1

    fan(NZ - 1, z_peer, lambda i: f_z.at[z_at(i)], lambda i: f_zrecv.at[i], f_send, f_recv, f_zrecv)

    g_cross(0)
    scores = g_score(1)
    scores = scores + g_score(0)
    p_part[...] = jnp.zeros_like(p_part)
    p_part[0, :, pl.ds(0, K)] = scores[0:8] + scores[8:16]
    push_one(p_part.at[0], p_recv.at[0], core_peer, p_send.at[0], p_recv_sem.at[0])
    take(p_recv.at[0], p_recv_sem.at[0])
    p_part[1] = p_part[0] + p_recv[0]
    push_one(p_part.at[1], p_recv.at[1], y_peer, p_send.at[1], p_recv_sem.at[1])
    take(p_recv.at[1], p_recv_sem.at[1])
    p_part[2] = p_part[1] + p_recv[1]
    fan(NZ - 1, z_peer, lambda i: p_part.at[2], lambda i: p_zrecv.at[i], p_send.at[2], p_recv_sem.at[2], p_zrecv)

    take(f_zrecv, f_recv)
    total = f_z[z].astype(F32)
    for i in range(NZ - 1):
        total += f_zrecv[i].astype(F32)
    group = s_all[1, z // 8, rows_of(z % 8, 16), :].astype(F32)
    place = 2 * y + c
    own = group[0:4]
    for n in range(1, 4):
        own = jnp.where(place == n, group[4 * n:4 * n + 4], own)
    for j in range(8):
        grad_ref[:, pl.ds(128 * j, 128)] = (own[:, 128 * j:128 * j + 128] + total[4 * j:4 * j + 4]).astype(BF16)

    take(p_zrecv, p_recv_sem.at[2])
    total = p_part[2]
    for i in range(NZ - 1):
        total += p_zrecv[i]
    score_ref[pl.ds(0, 1), :] = jnp.sum(total[0:4, :K], axis=0, keepdims=True)
    score_ref[pl.ds(1, 1), :] = jnp.sum(total[4:8, :K], axis=0, keepdims=True)

    for whole, sem in sent:
        take(whole, sem)


def on_device(activations, cotangent, up_weight, *others):
    operands = (activations, cotangent, jnp.swapaxes(up_weight, 1, 2)) + others
    dma, vmem = pltpu.SemaphoreType.DMA, pltpu.VMEM
    weight = vmem((W, D), BF16)
    scratch = [
        vmem((EX * M, D), BF16), vmem((EX * M, D), BF16), weight, weight, weight, weight,
        vmem((K, H), BF16), vmem((NZ, K, 4 * K), BF16), dma((12,)), dma((2, NZ // 2)), dma((2, NZ // 2)),
        vmem((4, EX, M, W), BF16), vmem((4, EX, T - 1, B, W), BF16), vmem((2, EX, M, W), BF16), vmem((EX, M, C_WIDTH), BF16),
        dma((2, 4, EX)), dma((2, 4, EX)), vmem((EX, B, W), F32),
        vmem((3, EX, M, D), BF16), vmem((3, EX, M // 2, D), BF16), vmem((3, EX, M // 4, D), BF16), vmem((3, EX, M // 4, D), BF16),
        vmem((2, EX, NZ, B, 128), BF16), vmem((2, EX, NZ - 1, B, 128), BF16), vmem((2, EX, M, D), BF16),
        dma((6, 3, EX)), dma((6, 3, EX)), vmem((EX, M, D), F32), vmem((EX, M // 4, D), F32),
        vmem((32, 128), F32), vmem((NZ, 32, 128), BF16), vmem((NZ - 1, 32, 128), BF16), dma, dma,
        vmem((2, 2, 2, 8, 8, 128), F32), vmem((2, 2, 8, 8, 128), F32), vmem((2, 2, 8, 8, 128), F32), vmem((2, 8, 8, 128), F32),
        dma((2, 2)), dma((2, 2)),
        vmem((3, 8, 128), F32), vmem((2, 8, 128), F32), vmem((NZ - 1, 8, 128), F32), dma((3,)), dma((3,)),
        vmem((4, EX, M, K), BF16), vmem((4, EX, M, K), BF16),
    ]
    return pl.pallas_call(
        kernel,
        name="window",
        out_shape=(jax.ShapeDtypeStruct((EX, K), F32), jax.ShapeDtypeStruct((4, D), BF16)),
        in_specs=[pl.BlockSpec(memory_space=pltpu.HBM)] * 7,
        out_specs=(pl.BlockSpec(memory_space=pltpu.VMEM), pl.BlockSpec(memory_space=pltpu.VMEM)),
        scratch_shapes=scratch,
        compiler_params=pltpu.CompilerParams(collective_id=0, has_side_effects=True, vmem_limit_bytes=60 << 20),
        cost_estimate=pl.CostEstimate(flops=2 * 10**9, bytes_accessed=5 * 10**6, transcendentals=0),
    )(*operands)


def solution(mesh):
    placed = (
        P(None, "tensor"),
        P(None, "tensor"),
        P(None, "tensor", "section"),
        P(None, "section", "tensor"),
        P(None, "tensor"),
        P(None, "section"),
        P("tensor", "section"),
    )
    return jax.shard_map(
        on_device,
        mesh=mesh,
        in_specs=placed,
        out_specs=(P(None, "tensor"), P("section", "tensor")),
        check_vma=False,
    )
```

```python
import functools

import jax
import jax.numpy as jnp
from jax import lax
from jax.experimental import pallas as pl
from jax.experimental.pallas import tpu as pltpu
from jax.sharding import PartitionSpec as P

MESH = pl.DeviceIdType.MESH
F32, BF16 = jnp.float32, jnp.bfloat16
EX = 2
M = 128
T = 8
NZ = 16
B = M // T
D = 1024
H = 448
K = 64
W = H + K
C_WIDTH = W + 2 * K


def silu_slope(values):
    sigma = jax.nn.sigmoid(values)
    return sigma * (1.0 + values * (1.0 - sigma))


def dot(a, b):
    return jnp.dot(a, b, preferred_element_type=F32)


def against(a, b):
    return lax.dot_general(a, b, (((1,), (1,)), ((), ())), preferred_element_type=F32)


def take(ref, sem):
    pltpu.make_async_copy(ref, ref, sem).wait()


def kernel(
    act_hbm, cot_hbm, up_hbm, down_hbm, width_hbm, hidden_hbm, query_hbm,
    score_ref, grad_ref,
    act, cot, up0, up1, dn0, dn1, hid, q_all, load_sem, q_send, q_recv,
    t_part, t_got, t_all, c_all, t_send, t_recv, pre_one,
    s_part, s_core, s_near, s_nrecv, s_far, s_frecv, s_all, s_send, s_recv, full32,
    f_turn, f_near, f_nrecv, f_far, f_frecv, f_send, f_recv, g_part, g_core, g_sum, g_yrecv, g_send, g_recv,
    p_part, p_recv, p_zrecv, p_send, p_recv_sem,
    left, right, score_part,
):
    s = lax.axis_index("section")
    t = lax.axis_index("tensor")
    z, y, c = s // 4, (s // 2) % 2, s % 2

    def section(zz, yy, cc):
        return {"section": zz * 4 + yy * 2 + cc}

    core_peer = section(z, y, 1 - c)
    y_peer = section(z, 1 - y, c)

    def z_at(i):
        far = (i + 1) // 2
        return lax.rem(z + 8 + jnp.where(i % 2 == 0, far, -far), NZ)

    def z_peer(i):
        return section(z_at(i), y, c)

    def t_at(i):
        return t ^ (i + 1)

    def t_peer(i):
        return {"tensor": t_at(i)}

    loads = {}

    def load(name, pairs, slot):
        copies = [pltpu.make_async_copy(a, b, load_sem.at[slot + n]) for n, (a, b) in enumerate(pairs)]
        for one in copies:
            one.start()
        loads[name] = copies

    def ready(name):
        for one in loads.pop(name, ()):
            one.wait()

    def weight(name, ref, buf, slot):
        load(name, [(ref, buf.at[pl.ds(0, H)]), (width_hbm, buf.at[pl.ds(H, K)])], slot)

    load("act", [(act_hbm, act)], 0)
    weight("up0", up_hbm.at[0], up0, 1)
    load("cot", [(cot_hbm, cot)], 3)
    weight("dn1", down_hbm.at[1], dn1, 4)
    weight("dn0", down_hbm.at[0], dn0, 6)
    load("hid", [(hidden_hbm, hid)], 8)
    load("qry", [(query_hbm, q_all.at[z])], 9)
    weight("up1", up_hbm.at[1], up1, 10)

    barrier = pltpu.get_barrier_semaphore()

    def greet(device):
        pl.semaphore_signal(barrier, inc=1, device_id=device, device_id_type=MESH)

    def greet_many(n, peer):
        def one(i, carry):
            greet(peer(i))
            return carry
        lax.fori_loop(0, n, one, 0)

    greet_many(NZ - 1, z_peer)
    greet_many(T - 1, t_peer)
    greet(y_peer)
    greet(core_peer)

    sent = []

    def push(src, dst, peer, send_sem, recv_sem):
        pltpu.make_async_remote_copy(
            src_ref=src, dst_ref=dst, send_sem=send_sem, recv_sem=recv_sem,
            device_id=peer, device_id_type=MESH,
        ).start()

    def fan(n, peer, src, dst, send_sem, recv_sem, whole):
        def one(i, carry):
            push(src(i), dst(i), peer(i), send_sem, recv_sem)
            return carry
        lax.fori_loop(0, n, one, 0)
        sent.append((whole, send_sem))

    def push_one(src, dst, peer, send_sem, recv_sem):
        push(src, dst, peer, send_sem, recv_sem)
        sent.append((dst, send_sem))

    steps = []

    def q_step():
        k = len(steps)
        if k == 0:
            ready("qry")
        for way in range(2):
            if 0 < k and (k < NZ // 2 or way == 0):
                take(q_all.at[0], q_recv.at[way, k - 1])
        steps.append(k)
        if k == NZ // 2:
            return
        for way, sign in enumerate((1, -1)):
            if k < NZ // 2 - 1 or way == 0:
                block = q_all.at[lax.rem(z - sign * k + NZ, NZ)]
                push_one(block, block, section(lax.rem(z + sign + NZ, NZ), y, c), q_send.at[way, k], q_recv.at[way, k])

    rows_of = lambda i, n: pl.ds(pl.multiple_of(i * n, n), n)

    def t_scatter(x, h):
        fan(
            T - 1, t_peer,
            lambda i: t_part.at[x, h, rows_of(t_at(i), B)],
            lambda i: t_got.at[x, h, i],
            t_send.at[0, x, h], t_recv.at[0, x, h], t_got.at[x, h],
        )

    def t_total(x, h):
        take(t_got.at[x, h], t_recv.at[0, x, h])
        total = t_part[x, h, rows_of(t, B), :].astype(F32)
        for i in range(T - 1):
            total += t_got[x, h, i].astype(F32)
        return total

    def t_gather(x, h, buf):
        mine = buf.at[h, rows_of(t, B)]
        others = buf.at[h, pl.ds(0, B * (T - 1))]
        fan(T - 1, t_peer, lambda i: mine, lambda i: mine, t_send.at[1, x, h], t_recv.at[1, x, h], others)
        return others

    near, far = z % 4, z // 4
    hops = [(2, 1), (-1, 1), (1, 1), (2, 0), (-1, 0), (1, 0), (0, 1)]

    def near_of(o, flip):
        zz, yy = lax.rem(z + o + NZ, NZ), (1 - y if flip else y)
        return yy, zz % 4, section(zz, yy, c)

    def far_of(k):
        return lax.rem(far + k, 4), section(lax.rem(z + 4 * k, NZ), y, c)

    def swap(p, h, value):
        full32[h] = value
        s_part[p, h] = value.astype(BF16)
        push_one(s_part.at[p, h, rows_of(1 - c, M // 2)], s_core.at[p, h], core_peer, s_send.at[0, p, h], s_recv.at[0, p, h])

    def swapped(p, h):
        take(s_core.at[p, h], s_recv.at[0, p, h])
        return full32[h, rows_of(c, M // 2), :] + s_core[p, h].astype(F32)

    def near_start(part, got, send_sem, recv_sem):
        for i, (o, flip) in enumerate(hops):
            yy, zm, peer = near_of(o, flip)
            push(part.at[yy, zm], got.at[i], peer, send_sem, recv_sem)
        sent.append((got, send_sem))

    def near_total(part, got, recv_sem):
        take(got, recv_sem)
        total = part[y, near].astype(F32)
        for i in range(len(hops)):
            total += got[i].astype(F32)
        return total

    half_row = pl.multiple_of(c * (M // 2), M // 2)
    tile_row = pl.multiple_of(half_row + (2 * y + near // 2) * B, B)
    tile_col = pl.multiple_of((near % 2) * (D // 2), D // 2)

    def s_sum(p, h, base):
        value = swapped(p, h)
        part, got = s_near.at[p, h], s_nrecv.at[p, h]
        for yy in range(2):
            for zm in range(4):
                at_row, at_col = (2 * yy + zm // 2) * B, (zm % 2) * (D // 2)
                part[yy, zm] = value[at_row:at_row + B, at_col:at_col + D // 2].astype(BF16)
        near_start(part, got, s_send.at[1, p, h], s_recv.at[1, p, h])
        yield
        s_far[p, h] = near_total(part, got, s_recv.at[1, p, h]).astype(BF16)
        for k in (2, 1, 3):
            push(s_far.at[p, h], s_frecv.at[p, h, k - 1], far_of(k)[1], s_send.at[2, p, h], s_recv.at[2, p, h])
        sent.append((s_frecv.at[p, h], s_send.at[2, p, h]))
        yield
        take(s_frecv.at[p, h], s_recv.at[2, p, h])
        total = s_far[p, h].astype(F32)
        for k in range(3):
            total += s_frecv[p, h, k].astype(F32)
        spot = s_all.at[p, h, pl.ds(tile_row, B), pl.ds(tile_col, D // 2)]
        s_all[p, h, pl.ds(tile_row, B), pl.ds(tile_col, D // 2)] = (tile_of(base, h) + total).astype(BF16)
        for o, flip in hops:
            push(spot, spot, near_of(o, flip)[2], s_send.at[3, p, h], s_recv.at[3, p, h])
        sent.append((got, s_send.at[3, p, h]))
        yield
        take(got, s_recv.at[3, p, h])
        half = s_all.at[p, h, pl.ds(half_row, M // 2)]
        push_one(half, half, core_peer, s_send.at[4, p, h], s_recv.at[4, p, h])
        yield
        take(half, s_recv.at[4, p, h])

    def tile_of(ref, h):
        return ref[pl.ds(pl.multiple_of(h * M + tile_row, B), B), pl.ds(tile_col, D // 2)].astype(F32)

    def spread(h):
        q = lax.broadcasted_iota(jnp.int32, (2 * K, K), 0)
        a = lax.broadcasted_iota(jnp.int32, (2 * K, K), 1)
        pick = (a == (q // 8) * 4 + q % 4) & ((q // 4) % 2 == h)
        return jnp.where(pick, 1.0, 0.0).astype(BF16)

    def keep(m, h, value):
        left[m, :, pl.ds(h * M, M)] = against(spread(h), value).astype(BF16)

    def products(m):
        total = dot(left[m], right[m])
        for i in range(16):
            g_part[m // 2, i % 2, (i // 2) % 2, 4 * (m % 2) + i // 4, :, pl.ds(0, K)] = total[8 * i:8 * i + 8]

    def g_swap(u):
        products(2 * u)
        products(2 * u + 1)
        push_one(g_part.at[u, 1 - c], g_core.at[u], core_peer, g_send.at[0, u], g_recv.at[0, u])

    def g_cross(u):
        take(g_core.at[u], g_recv.at[0, u])
        g_sum[u] = g_part[u, c] + g_core[u]
        push_one(g_sum.at[u, 1 - y], g_yrecv.at[u], y_peer, g_send.at[1, u], g_recv.at[1, u])

    at_row = lax.broadcasted_iota(jnp.int32, (8, 4 * K), 0) % 4
    at_lane = lax.broadcasted_iota(jnp.int32, (8, 4 * K), 1) // K

    def g_score(u):
        take(g_yrecv.at[u], g_recv.at[1, u])
        total = jnp.zeros((16, K), F32)
        for i in range(8):
            one = (g_sum[u, y, i] + g_yrecv[u, i])[:, :K]
            wide = jnp.where(at_row == at_lane, jnp.concatenate([one, one, one, one], axis=1), 0.0)
            high = wide.astype(BF16).astype(F32)
            both = jnp.concatenate([high, wide - high], axis=0).astype(BF16)
            total += against(both, q_all[8 * u + i])
        return total

    def stream(h):
        rows = slice(h * M, h * M + M)
        lanes = lax.broadcasted_iota(jnp.int32, (B, W), 1)
        if h == 0:
            ready("act")
            ready("up0")
        t_part[0, h] = against(act[rows], up0[...]).astype(BF16)
        if h == 0:
            pl.semaphore_wait(barrier, NZ - 1 + T - 1 + 2)
        t_scatter(0, h)
        yield
        if h == 0:
            ready("cot")
            ready("dn1")
        t_part[1, h] = against(cot[rows], dn1[...]).astype(BF16)
        t_scatter(1, h)
        total = t_total(0, h)
        pre_one[h] = total
        t_all[0, h, rows_of(t, B), :] = jnp.where(lanes < H, jax.nn.silu(total), total).astype(BF16)
        others = t_gather(0, h, t_all.at[0])
        yield
        if h == 0:
            ready("dn0")
            ready("hid")
        take(others, t_recv.at[1, 0, h])
        act_one = t_all[0, h, :, pl.ds(0, H)]
        swap(0, h, dot(act_one, dn0[pl.ds(0, H), :]))
        keep(0, h, t_all[0, h, :, pl.ds(H, K)])
        keep(1, h, against(act_one, hid[...]).astype(BF16))
        yield
        yield from s_sum(0, h, act)
        if h == 0:
            ready("up1")
        resid = s_all[0, h]
        t_part[2, h] = against(resid, up1[...]).astype(BF16)
        t_scatter(2, h)
        back = t_total(1, h)
        yield
        total = t_total(2, h)
        act_two = jax.nn.silu(total[:, :H]).astype(BF16)
        own = rows_of(t, B)
        c_all[h, own, pl.ds(0, W)] = jnp.where(lanes < H, back * silu_slope(total), total).astype(BF16)
        c_all[h, own, pl.ds(W, K)] = against(act_two, hid[...]).astype(BF16)
        c_all[h, own, pl.ds(W + K, K)] = back[:, H:].astype(BF16)
        others = t_gather(2, h, c_all)
        yield
        take(others, t_recv.at[1, 2, h])
        delta_two = c_all[h, :, pl.ds(0, H)]
        swap(1, h, dot(delta_two, up1[pl.ds(0, H), :]))
        keep(2, h, c_all[h, :, pl.ds(H, K)])
        keep(3, h, c_all[h, :, pl.ds(W, K)])
        right[3, rows, :] = c_all[h, :, pl.ds(W + K, K)]
        right[2, rows, :] = against(delta_two, hid[...]).astype(BF16)
        yield
        yield from s_sum(1, h, cot)
        t_part[3, h] = against(s_all[1, h], dn0[...]).astype(BF16)
        t_scatter(3, h)
        if h == 1:
            g_swap(1)
        yield
        total = t_total(3, h)
        t_all[1, h, rows_of(t, B), :] = jnp.where(lanes < H, total * silu_slope(pre_one[h]), total).astype(BF16)
        others = t_gather(3, h, t_all.at[1])
        if h == 1:
            g_cross(1)
        yield
        take(others, t_recv.at[1, 3, h])
        delta_one = t_all[1, h, :, pl.ds(0, H)]
        right[1, rows, :] = t_all[1, h, :, pl.ds(H, K)]
        right[0, rows, :] = against(delta_one, hid[...]).astype(BF16)
        if h == 1:
            g_swap(0)
        to = lax.broadcasted_iota(jnp.int32, (M, M), 0)
        came = lax.broadcasted_iota(jnp.int32, (M, M), 1)
        source = (((to // 4) % 2) * 4 + (to // 8) % 4) * 16 + ((to // 32) % 2) * 8 + (to // 64) * 4 + to % 4
        turn = jnp.where(came == source, 1.0, 0.0).astype(BF16)
        turned = dot(turn, delta_one).astype(BF16)
        swap(2, h, dot(turned, up0[pl.ds(0, H), :]))
        if h == 0:
            score_part[...] = g_score(1)
        else:
            g_cross(0)
        yield
        value = swapped(2, h)
        for n in range(16):
            for j in range(8):
                f_turn[h, n, pl.ds(4 * j, 4), :] = value[4 * n:4 * n + 4, 128 * j:128 * j + 128]
        for n in range(8):
            f_near[h, n // 4, n % 4] = jnp.concatenate([f_turn[h, 2 * n], f_turn[h, 2 * n + 1]], axis=0).astype(BF16)
        near_start(f_near.at[h], f_nrecv.at[h], f_send.at[h], f_recv.at[h])
        yield
        total = near_total(f_near.at[h], f_nrecv.at[h], f_recv.at[h])
        f_far[2 * h] = total[0:32].astype(BF16)
        f_far[2 * h + 1] = total[32:64].astype(BF16)

    streams = [stream(h) for h in range(EX)]
    g_part[...] = jnp.zeros_like(g_part)
    turns = 0
    while streams:
        for one in list(streams):
            try:
                next(one)
            except StopIteration:
                streams.remove(one)
        if turns <= NZ // 2:
            q_step()
        turns += 1

    for k in (2, 1, 3):
        to_far, peer = far_of(k)
        push(f_far.at[to_far], f_frecv.at[k - 1], peer, f_send.at[2], f_recv.at[2])
    sent.append((f_frecv, f_send.at[2]))

    scores = score_part[...] + g_score(0)
    p_part[...] = jnp.zeros_like(p_part)
    p_part[0, :, pl.ds(0, K)] = scores[0:8] + scores[8:16]
    push_one(p_part.at[0], p_recv.at[0], core_peer, p_send.at[0], p_recv_sem.at[0])
    take(p_recv.at[0], p_recv_sem.at[0])
    p_part[1] = p_part[0] + p_recv[0]
    push_one(p_part.at[1], p_recv.at[1], y_peer, p_send.at[1], p_recv_sem.at[1])
    take(p_recv.at[1], p_recv_sem.at[1])
    p_part[2] = p_part[1] + p_recv[1]
    fan(NZ - 1, z_peer, lambda i: p_part.at[2], lambda i: p_zrecv.at[i], p_send.at[2], p_recv_sem.at[2], p_zrecv)

    take(f_frecv, f_recv.at[2])
    total = f_far[far].astype(F32)
    for k in range(3):
        total += f_frecv[k].astype(F32)
    group = s_all[1, z // 8, rows_of(z % 8, 16), :].astype(F32)
    place = 2 * y + c
    own = group[0:4]
    for n in range(1, 4):
        own = jnp.where(place == n, group[4 * n:4 * n + 4], own)
    for j in range(8):
        grad_ref[:, pl.ds(128 * j, 128)] = (own[:, 128 * j:128 * j + 128] + total[4 * j:4 * j + 4]).astype(BF16)

    take(p_zrecv, p_recv_sem.at[2])
    total = p_part[2]
    for i in range(NZ - 1):
        total += p_zrecv[i]
    score_ref[pl.ds(0, 1), :] = jnp.sum(total[0:4, :K], axis=0, keepdims=True)
    score_ref[pl.ds(1, 1), :] = jnp.sum(total[4:8, :K], axis=0, keepdims=True)

    for whole, sem in sent:
        take(whole, sem)


def hand_over(score_in, grad_in, score_ref, grad_ref):
    score_ref[...] = score_in[...]
    grad_ref[...] = grad_in[...]


def on_device(activations, cotangent, up_weight, *others):
    operands = (activations, cotangent, jnp.swapaxes(up_weight, 1, 2)) + others
    dma, vmem = pltpu.SemaphoreType.DMA, pltpu.VMEM
    weight = vmem((W, D), BF16)
    scratch = [
        vmem((EX * M, D), BF16), vmem((EX * M, D), BF16), weight, weight, weight, weight,
        vmem((K, H), BF16), vmem((NZ, K, 4 * K), BF16), dma((12,)), dma((2, NZ // 2)), dma((2, NZ // 2)),
        vmem((4, EX, M, W), BF16), vmem((4, EX, T - 1, B, W), BF16), vmem((2, EX, M, W), BF16), vmem((EX, M, C_WIDTH), BF16),
        dma((2, 4, EX)), dma((2, 4, EX)), vmem((EX, B, W), F32),
        vmem((3, EX, M, D), BF16), vmem((3, EX, M // 2, D), BF16), vmem((2, EX, 2, 4, B, D // 2), BF16), vmem((2, EX, 7, B, D // 2), BF16),
        vmem((2, EX, B, D // 2), BF16), vmem((2, EX, 3, B, D // 2), BF16), vmem((2, EX, M, D), BF16),
        dma((5, 3, EX)), dma((5, 3, EX)), vmem((EX, M, D), F32),
        vmem((EX, 16, 32, 128), F32), vmem((EX, 2, 4, 64, 128), BF16), vmem((EX, 7, 64, 128), BF16),
        vmem((4, 32, 128), BF16), vmem((3, 32, 128), BF16), dma((3,)), dma((3,)),
        vmem((2, 2, 2, 8, 8, 128), F32), vmem((2, 2, 8, 8, 128), F32), vmem((2, 2, 8, 8, 128), F32), vmem((2, 8, 8, 128), F32),
        dma((2, 2)), dma((2, 2)),
        vmem((3, 8, 128), F32), vmem((2, 8, 128), F32), vmem((NZ - 1, 8, 128), F32), dma((3,)), dma((3,)),
        vmem((4, 2 * K, EX * M), BF16), vmem((4, EX * M, K), BF16), vmem((16, K), F32),
    ]
    results = pl.pallas_call(
        kernel,
        name="window",
        out_shape=(jax.ShapeDtypeStruct((EX, K), F32), jax.ShapeDtypeStruct((4, D), BF16)),
        in_specs=[pl.BlockSpec(memory_space=pltpu.HBM)] * 7,
        out_specs=(pl.BlockSpec(memory_space=pltpu.VMEM), pl.BlockSpec(memory_space=pltpu.VMEM)),
        scratch_shapes=scratch,
        compiler_params=pltpu.CompilerParams(collective_id=0, has_side_effects=True, vmem_limit_bytes=60 << 20),
        cost_estimate=pl.CostEstimate(flops=2 * 10**9, bytes_accessed=5 * 10**6, transcendentals=0),
    )(*operands)
    whole = [pl.BlockSpec(memory_space=pltpu.VMEM)] * 2
    return pl.pallas_call(
        hand_over,
        name="hand_over",
        out_shape=tuple(jax.ShapeDtypeStruct(r.shape, r.dtype) for r in results),
        in_specs=whole,
        out_specs=tuple(whole),
    )(*results)


def solution(mesh):
    placed = (
        P(None, "tensor"),
        P(None, "tensor"),
        P(None, "tensor", "section"),
        P(None, "section", "tensor"),
        P(None, "tensor"),
        P(None, "section"),
        P("tensor", "section"),
    )
    return jax.shard_map(
        on_device,
        mesh=mesh,
        in_specs=placed,
        out_specs=(P(None, "tensor"), P("section", "tensor")),
        check_vma=False,
    )
```

```python
import functools

import jax
import jax.numpy as jnp
from jax import lax
from jax.experimental import pallas as pl
from jax.experimental.pallas import tpu as pltpu
from jax.sharding import PartitionSpec as P

MESH = pl.DeviceIdType.MESH
F32, BF16 = jnp.float32, jnp.bfloat16
EX = 2
M = 128
T = 8
NZ = 16
B = M // T
D = 1024
H = 448
K = 64
W = H + K
C_WIDTH = W + 2 * K


def silu_slope(values):
    sigma = jax.nn.sigmoid(values)
    return sigma * (1.0 + values * (1.0 - sigma))


def dot(a, b):
    return jnp.dot(a, b, preferred_element_type=F32)


def against(a, b):
    return lax.dot_general(a, b, (((1,), (1,)), ((), ())), preferred_element_type=F32)


def take(ref, sem):
    pltpu.make_async_copy(ref, ref, sem).wait()


def kernel(
    act_hbm, cot_hbm, up_hbm, down_hbm, width_hbm, hidden_hbm, query_hbm,
    score_ref, grad_ref,
    act, cot, up0, up1, dn0, dn1, hid, q_all, load_sem, q_send, q_recv,
    t_part, t_got, t_all, c_all, t_send, t_recv, pre_one,
    s_part, s_core, s_near, s_nrecv, s_far, s_frecv, s_all, s_send, s_recv, full32,
    f_turn, f_near, f_nrecv, f_far, f_frecv, f_send, f_recv, g_part, g_core, g_sum, g_yrecv, g_send, g_recv,
    p_part, p_recv, p_zrecv, p_send, p_recv_sem,
    left, right, score_part,
):
    s = lax.axis_index("section")
    t = lax.axis_index("tensor")
    z, y, c = s // 4, (s // 2) % 2, s % 2

    def section(zz, yy, cc):
        return {"section": zz * 4 + yy * 2 + cc}

    core_peer = section(z, y, 1 - c)
    y_peer = section(z, 1 - y, c)

    def z_at(i):
        far = (i + 1) // 2
        return lax.rem(z + 8 + jnp.where(i % 2 == 0, far, -far), NZ)

    def z_peer(i):
        return section(z_at(i), y, c)

    def t_at(i):
        return t ^ (i + 1)

    def t_peer(i):
        return {"tensor": t_at(i)}

    loads = {}

    def load(name, pairs, slot):
        copies = [pltpu.make_async_copy(a, b, load_sem.at[slot + n]) for n, (a, b) in enumerate(pairs)]
        for one in copies:
            one.start()
        loads[name] = copies

    def ready(name):
        for one in loads.pop(name, ()):
            one.wait()

    def weight(name, ref, buf, slot):
        load(name, [(ref, buf.at[pl.ds(0, H)]), (width_hbm, buf.at[pl.ds(H, K)])], slot)

    load("act", [(act_hbm, act)], 0)
    weight("up0", up_hbm.at[0], up0, 1)
    load("cot", [(cot_hbm, cot)], 3)
    weight("dn1", down_hbm.at[1], dn1, 4)
    weight("dn0", down_hbm.at[0], dn0, 6)
    load("hid", [(hidden_hbm, hid)], 8)
    load("qry", [(query_hbm, q_all.at[z])], 9)
    weight("up1", up_hbm.at[1], up1, 10)

    barrier = pltpu.get_barrier_semaphore()

    def greet(device):
        pl.semaphore_signal(barrier, inc=1, device_id=device, device_id_type=MESH)

    def greet_many(n, peer):
        def one(i, carry):
            greet(peer(i))
            return carry
        lax.fori_loop(0, n, one, 0)

    greet_many(NZ - 1, z_peer)
    greet_many(T - 1, t_peer)
    greet(y_peer)
    greet(core_peer)
    for o in (-2, -1, 1, 2):
        greet(section(lax.rem(z + o + NZ, NZ), 1 - y, c))

    sent = []

    def push(src, dst, peer, send_sem, recv_sem):
        pltpu.make_async_remote_copy(
            src_ref=src, dst_ref=dst, send_sem=send_sem, recv_sem=recv_sem,
            device_id=peer, device_id_type=MESH,
        ).start()

    def fan(n, peer, src, dst, send_sem, recv_sem, whole):
        def one(i, carry):
            push(src(i), dst(i), peer(i), send_sem, recv_sem)
            return carry
        lax.fori_loop(0, n, one, 0)
        sent.append((whole, send_sem))

    def push_one(src, dst, peer, send_sem, recv_sem):
        push(src, dst, peer, send_sem, recv_sem)
        sent.append((dst, send_sem))

    steps = []

    def q_step():
        k = len(steps)
        if k == 0:
            ready("qry")
        for way in range(2):
            if 0 < k and (k < NZ // 2 or way == 0):
                take(q_all.at[0], q_recv.at[way, k - 1])
        steps.append(k)
        if k == NZ // 2:
            return
        for way, sign in enumerate((1, -1)):
            if k < NZ // 2 - 1 or way == 0:
                block = q_all.at[lax.rem(z - sign * k + NZ, NZ)]
                push_one(block, block, section(lax.rem(z + sign + NZ, NZ), y, c), q_send.at[way, k], q_recv.at[way, k])

    rows_of = lambda i, n: pl.ds(pl.multiple_of(i * n, n), n)

    def t_scatter(x, h):
        fan(
            T - 1, t_peer,
            lambda i: t_part.at[x, h, rows_of(t_at(i), B)],
            lambda i: t_got.at[x, h, i],
            t_send.at[0, x, h], t_recv.at[0, x, h], t_got.at[x, h],
        )

    def t_total(x, h):
        take(t_got.at[x, h], t_recv.at[0, x, h])
        total = t_part[x, h, rows_of(t, B), :].astype(F32)
        for i in range(T - 1):
            total += t_got[x, h, i].astype(F32)
        return total

    def t_gather(x, h, buf):
        mine = buf.at[h, rows_of(t, B)]
        others = buf.at[h, pl.ds(0, B * (T - 1))]
        fan(T - 1, t_peer, lambda i: mine, lambda i: mine, t_send.at[1, x, h], t_recv.at[1, x, h], others)
        return others

    near, far = z % 4, z // 4
    hops = [(2, 1), (-1, 1), (1, 1), (2, 0), (-1, 0), (1, 0), (0, 1)]

    def near_of(o, flip):
        zz, yy = lax.rem(z + o + NZ, NZ), (1 - y if flip else y)
        return yy, zz % 4, section(zz, yy, c)

    across = lax.rem(near + 2, 4)
    strides = (6, -6, 2, -2)

    def swap(p, h, value):
        full32[h] = value
        s_part[p, h] = value.astype(BF16)
        push_one(s_part.at[p, h, rows_of(1 - c, M // 2)], s_core.at[p, h], core_peer, s_send.at[0, p, h], s_recv.at[0, p, h])

    def swapped(p, h):
        take(s_core.at[p, h], s_recv.at[0, p, h])
        return full32[h, rows_of(c, M // 2), :] + s_core[p, h].astype(F32)

    def near_start(part, got, send_sem, recv_sem):
        for i, (o, flip) in enumerate(hops):
            yy, zm, peer = near_of(o, flip)
            push(part.at[yy, zm], got.at[i], peer, send_sem, recv_sem)
        sent.append((got, send_sem))

    def near_total(part, got, recv_sem):
        take(got, recv_sem)
        total = part[y, near].astype(F32)
        for i in range(len(hops)):
            total += got[i].astype(F32)
        return total

    half_row = pl.multiple_of(c * (M // 2), M // 2)
    tile_row = pl.multiple_of(half_row + (2 * y + across // 2) * B, B)
    tile_col = pl.multiple_of((across % 2) * (D // 2), D // 2)

    def s_sum(p, h, base):
        value = swapped(p, h)
        part, got = s_near.at[p, h], s_nrecv.at[p, h]
        for yy in range(2):
            for zm in range(4):
                at_row, at_col = (2 * yy + zm // 2) * B, (zm % 2) * (D // 2)
                part[yy, zm] = value[at_row:at_row + B, at_col:at_col + D // 2].astype(BF16)
        near_start(part, got, s_send.at[1, p, h], s_recv.at[1, p, h])
        yield
        s_far[p, h] = near_total(part, got, s_recv.at[1, p, h]).astype(BF16)
        for i, o in enumerate(strides):
            peer = section(lax.rem(z + o + NZ, NZ), y, c)
            push(s_far.at[p, h], s_frecv.at[p, h, i], peer, s_send.at[2, p, h], s_recv.at[2, p, h])
        sent.append((s_frecv.at[p, h], s_send.at[2, p, h]))
        yield
        take(s_frecv.at[p, h], s_recv.at[2, p, h])
        total = s_frecv[p, h, 0].astype(F32)
        for i in range(1, 4):
            total += s_frecv[p, h, i].astype(F32)
        spot = s_all.at[p, h, pl.ds(tile_row, B), pl.ds(tile_col, D // 2)]
        s_all[p, h, pl.ds(tile_row, B), pl.ds(tile_col, D // 2)] = (tile_of(base, h) + total).astype(BF16)
        for o, flip in hops:
            push(spot, spot, near_of(o, flip)[2], s_send.at[3, p, h], s_recv.at[3, p, h])
        sent.append((got, s_send.at[3, p, h]))
        yield
        take(got, s_recv.at[3, p, h])
        half = s_all.at[p, h, pl.ds(half_row, M // 2)]
        push_one(half, half, core_peer, s_send.at[4, p, h], s_recv.at[4, p, h])
        yield
        take(half, s_recv.at[4, p, h])

    def tile_of(ref, h):
        return ref[pl.ds(pl.multiple_of(h * M + tile_row, B), B), pl.ds(tile_col, D // 2)].astype(F32)

    def spread(h):
        q = lax.broadcasted_iota(jnp.int32, (2 * K, K), 0)
        a = lax.broadcasted_iota(jnp.int32, (2 * K, K), 1)
        pick = (a == (q // 8) * 4 + q % 4) & ((q // 4) % 2 == h)
        return jnp.where(pick, 1.0, 0.0).astype(BF16)

    def keep(m, h, value):
        left[m, :, pl.ds(h * M, M)] = against(spread(h), value).astype(BF16)

    def products(m):
        total = dot(left[m], right[m])
        for i in range(16):
            g_part[m // 2, i % 2, (i // 2) % 2, 4 * (m % 2) + i // 4, :, pl.ds(0, K)] = total[8 * i:8 * i + 8]

    def g_swap(u):
        products(2 * u)
        products(2 * u + 1)
        push_one(g_part.at[u, 1 - c], g_core.at[u], core_peer, g_send.at[0, u], g_recv.at[0, u])

    def g_cross(u):
        take(g_core.at[u], g_recv.at[0, u])
        g_sum[u] = g_part[u, c] + g_core[u]
        push_one(g_sum.at[u, 1 - y], g_yrecv.at[u], y_peer, g_send.at[1, u], g_recv.at[1, u])

    at_row = lax.broadcasted_iota(jnp.int32, (8, 4 * K), 0) % 4
    at_lane = lax.broadcasted_iota(jnp.int32, (8, 4 * K), 1) // K

    def g_score(u):
        take(g_yrecv.at[u], g_recv.at[1, u])
        total = jnp.zeros((16, K), F32)
        for i in range(8):
            one = (g_sum[u, y, i] + g_yrecv[u, i])[:, :K]
            wide = jnp.where(at_row == at_lane, jnp.concatenate([one, one, one, one], axis=1), 0.0)
            high = wide.astype(BF16).astype(F32)
            both = jnp.concatenate([high, wide - high], axis=0).astype(BF16)
            total += against(both, q_all[8 * u + i])
        return total

    def stream(h):
        rows = slice(h * M, h * M + M)
        lanes = lax.broadcasted_iota(jnp.int32, (B, W), 1)
        if h == 0:
            ready("act")
            ready("up0")
        t_part[0, h] = against(act[rows], up0[...]).astype(BF16)
        if h == 0:
            pl.semaphore_wait(barrier, NZ - 1 + T - 1 + 2 + 4)
        t_scatter(0, h)
        yield
        if h == 0:
            ready("cot")
            ready("dn1")
        t_part[1, h] = against(cot[rows], dn1[...]).astype(BF16)
        total = t_total(0, h)
        pre_one[h] = total
        t_all[0, h, rows_of(t, B), :] = jnp.where(lanes < H, jax.nn.silu(total), total).astype(BF16)
        others = t_gather(0, h, t_all.at[0])
        yield
        if h == 0:
            ready("dn0")
            ready("hid")
        take(others, t_recv.at[1, 0, h])
        act_one = t_all[0, h, :, pl.ds(0, H)]
        swap(0, h, dot(act_one, dn0[pl.ds(0, H), :]))
        keep(0, h, t_all[0, h, :, pl.ds(H, K)])
        keep(1, h, against(act_one, hid[...]).astype(BF16))
        yield
        going = s_sum(0, h, act)
        next(going)
        t_scatter(1, h)
        yield
        yield from going
        if h == 0:
            ready("up1")
        resid = s_all[0, h]
        t_part[2, h] = against(resid, up1[...]).astype(BF16)
        t_scatter(2, h)
        back = t_total(1, h)
        yield
        total = t_total(2, h)
        act_two = jax.nn.silu(total[:, :H]).astype(BF16)
        own = rows_of(t, B)
        c_all[h, own, pl.ds(0, W)] = jnp.where(lanes < H, back * silu_slope(total), total).astype(BF16)
        c_all[h, own, pl.ds(W, K)] = against(act_two, hid[...]).astype(BF16)
        c_all[h, own, pl.ds(W + K, K)] = back[:, H:].astype(BF16)
        others = t_gather(2, h, c_all)
        yield
        take(others, t_recv.at[1, 2, h])
        delta_two = c_all[h, :, pl.ds(0, H)]
        swap(1, h, dot(delta_two, up1[pl.ds(0, H), :]))
        keep(2, h, c_all[h, :, pl.ds(H, K)])
        keep(3, h, c_all[h, :, pl.ds(W, K)])
        right[3, rows, :] = c_all[h, :, pl.ds(W + K, K)]
        right[2, rows, :] = against(delta_two, hid[...]).astype(BF16)
        yield
        yield from s_sum(1, h, cot)
        t_part[3, h] = against(s_all[1, h], dn0[...]).astype(BF16)
        t_scatter(3, h)
        if h == 1:
            g_swap(1)
        yield
        total = t_total(3, h)
        t_all[1, h, rows_of(t, B), :] = jnp.where(lanes < H, total * silu_slope(pre_one[h]), total).astype(BF16)
        others = t_gather(3, h, t_all.at[1])
        if h == 1:
            g_cross(1)
        yield
        take(others, t_recv.at[1, 3, h])
        delta_one = t_all[1, h, :, pl.ds(0, H)]
        right[1, rows, :] = t_all[1, h, :, pl.ds(H, K)]
        right[0, rows, :] = against(delta_one, hid[...]).astype(BF16)
        if h == 1:
            g_swap(0)
        to = lax.broadcasted_iota(jnp.int32, (M, M), 0)
        came = lax.broadcasted_iota(jnp.int32, (M, M), 1)
        source = (((to // 4) % 2) * 4 + (to // 8) % 4) * 16 + ((to // 32) % 2) * 8 + (to // 64) * 4 + to % 4
        turn = jnp.where(came == source, 1.0, 0.0).astype(BF16)
        turned = dot(turn, delta_one).astype(BF16)
        swap(2, h, dot(turned, up0[pl.ds(0, H), :]))
        if h == 0:
            score_part[...] = g_score(1)
        else:
            g_cross(0)
        yield
        value = swapped(2, h)
        for n in range(16):
            for j in range(8):
                f_turn[h, n, pl.ds(4 * j, 4), :] = value[4 * n:4 * n + 4, 128 * j:128 * j + 128]
        for n in range(8):
            f_near[h, n // 4, (n + 2) % 4] = jnp.concatenate([f_turn[h, 2 * n], f_turn[h, 2 * n + 1]], axis=0).astype(BF16)
        near_start(f_near.at[h], f_nrecv.at[h], f_send.at[h], f_recv.at[h])
        if h == 1:
            scores = score_part[...] + g_score(0)
            p_part[0, :, pl.ds(0, K)] = scores[0:8] + scores[8:16]
            push_one(p_part.at[0], p_recv.at[0], core_peer, p_send.at[0], p_recv_sem.at[0])
        yield
        if h == 1:
            take(p_recv.at[0], p_recv_sem.at[0])
            p_part[1] = p_part[0] + p_recv[0]
            push_one(p_part.at[1], p_recv.at[1], y_peer, p_send.at[1], p_recv_sem.at[1])
        total = near_total(f_near.at[h], f_nrecv.at[h], f_recv.at[h])
        for k in range(2):
            f_far[2 * h + k] = total[32 * k:32 * k + 32].astype(BF16)
            peer = section(4 * (2 * h + k) + across, y, c)
            push(f_far.at[2 * h + k], f_frecv.at[far], peer, f_send.at[2], f_recv.at[2])

    streams = [stream(h) for h in range(EX)]
    g_part[...] = jnp.zeros_like(g_part)
    p_part[...] = jnp.zeros_like(p_part)
    turns = 0
    while streams:
        for one in list(streams):
            try:
                next(one)
            except StopIteration:
                streams.remove(one)
        if turns <= NZ // 2:
            q_step()
        turns += 1

    sent.append((f_frecv, f_send.at[2]))
    take(p_recv.at[1], p_recv_sem.at[1])
    p_part[2] = p_part[1] + p_recv[1]
    fan(NZ - 1, z_peer, lambda i: p_part.at[2], lambda i: p_zrecv.at[i], p_send.at[2], p_recv_sem.at[2], p_zrecv)

    take(f_frecv, f_recv.at[2])
    total = f_frecv[0].astype(F32)
    for i in range(1, 4):
        total += f_frecv[i].astype(F32)
    group = s_all[1, z // 8, rows_of(z % 8, 16), :].astype(F32)
    place = 2 * y + c
    own = group[0:4]
    for n in range(1, 4):
        own = jnp.where(place == n, group[4 * n:4 * n + 4], own)
    for j in range(8):
        grad_ref[:, pl.ds(128 * j, 128)] = (own[:, 128 * j:128 * j + 128] + total[4 * j:4 * j + 4]).astype(BF16)

    take(p_zrecv, p_recv_sem.at[2])
    total = p_part[2]
    for i in range(NZ - 1):
        total += p_zrecv[i]
    score_ref[pl.ds(0, 1), :] = jnp.sum(total[0:4, :K], axis=0, keepdims=True)
    score_ref[pl.ds(1, 1), :] = jnp.sum(total[4:8, :K], axis=0, keepdims=True)

    for whole, sem in sent:
        take(whole, sem)


def hand_over(score_in, grad_in, score_ref, grad_ref):
    score_ref[...] = score_in[...]
    grad_ref[...] = grad_in[...]


def on_device(activations, cotangent, up_weight, *others):
    operands = (activations, cotangent, jnp.swapaxes(up_weight, 1, 2)) + others
    dma, vmem = pltpu.SemaphoreType.DMA, pltpu.VMEM
    weight = vmem((W, D), BF16)
    scratch = [
        vmem((EX * M, D), BF16), vmem((EX * M, D), BF16), weight, weight, weight, weight,
        vmem((K, H), BF16), vmem((NZ, K, 4 * K), BF16), dma((12,)), dma((2, NZ // 2)), dma((2, NZ // 2)),
        vmem((4, EX, M, W), BF16), vmem((4, EX, T - 1, B, W), BF16), vmem((2, EX, M, W), BF16), vmem((EX, M, C_WIDTH), BF16),
        dma((2, 4, EX)), dma((2, 4, EX)), vmem((EX, B, W), F32),
        vmem((3, EX, M, D), BF16), vmem((3, EX, M // 2, D), BF16), vmem((2, EX, 2, 4, B, D // 2), BF16), vmem((2, EX, 7, B, D // 2), BF16),
        vmem((2, EX, B, D // 2), BF16), vmem((2, EX, 4, B, D // 2), BF16), vmem((2, EX, M, D), BF16),
        dma((5, 3, EX)), dma((5, 3, EX)), vmem((EX, M, D), F32),
        vmem((EX, 16, 32, 128), F32), vmem((EX, 2, 4, 64, 128), BF16), vmem((EX, 7, 64, 128), BF16),
        vmem((4, 32, 128), BF16), vmem((4, 32, 128), BF16), dma((3,)), dma((3,)),
        vmem((2, 2, 2, 8, 8, 128), F32), vmem((2, 2, 8, 8, 128), F32), vmem((2, 2, 8, 8, 128), F32), vmem((2, 8, 8, 128), F32),
        dma((2, 2)), dma((2, 2)),
        vmem((3, 8, 128), F32), vmem((2, 8, 128), F32), vmem((NZ - 1, 8, 128), F32), dma((3,)), dma((3,)),
        vmem((4, 2 * K, EX * M), BF16), vmem((4, EX * M, K), BF16), vmem((16, K), F32),
    ]
    results = pl.pallas_call(
        kernel,
        name="window",
        out_shape=(jax.ShapeDtypeStruct((EX, K), F32), jax.ShapeDtypeStruct((4, D), BF16)),
        in_specs=[pl.BlockSpec(memory_space=pltpu.HBM)] * 7,
        out_specs=(pl.BlockSpec(memory_space=pltpu.VMEM), pl.BlockSpec(memory_space=pltpu.VMEM)),
        scratch_shapes=scratch,
        compiler_params=pltpu.CompilerParams(collective_id=0, has_side_effects=True, vmem_limit_bytes=60 << 20),
        cost_estimate=pl.CostEstimate(flops=2 * 10**9, bytes_accessed=5 * 10**6, transcendentals=0),
    )(*operands)
    whole = [pl.BlockSpec(memory_space=pltpu.VMEM)] * 2
    return pl.pallas_call(
        hand_over,
        name="hand_over",
        out_shape=tuple(jax.ShapeDtypeStruct(r.shape, r.dtype) for r in results),
        in_specs=whole,
        out_specs=tuple(whole),
    )(*results)


def solution(mesh):
    placed = (
        P(None, "tensor"),
        P(None, "tensor"),
        P(None, "tensor", "section"),
        P(None, "section", "tensor"),
        P(None, "tensor"),
        P(None, "section"),
        P("tensor", "section"),
    )
    return jax.shard_map(
        on_device,
        mesh=mesh,
        in_specs=placed,
        out_specs=(P(None, "tensor"), P("section", "tensor")),
        check_vma=False,
    )
```

```python
import functools

import jax
import jax.numpy as jnp
from jax import lax
from jax.experimental import pallas as pl
from jax.experimental.pallas import tpu as pltpu
from jax.sharding import PartitionSpec as P

MESH = pl.DeviceIdType.MESH
F32, BF16 = jnp.float32, jnp.bfloat16
EX = 2
M = 128
T = 8
NZ = 16
B = M // T
D = 1024
H = 448
K = 64
W = H + K
C_WIDTH = W + 2 * K


def silu_slope(values):
    sigma = jax.nn.sigmoid(values)
    return sigma * (1.0 + values * (1.0 - sigma))


def dot(a, b):
    return jnp.dot(a, b, preferred_element_type=F32)


def against(a, b):
    return lax.dot_general(a, b, (((1,), (1,)), ((), ())), preferred_element_type=F32)


def take(ref, sem):
    pltpu.make_async_copy(ref, ref, sem).wait()


def kernel(
    act_hbm, cot_hbm, up_hbm, down_hbm, width_hbm, hidden_hbm, query_hbm,
    score_ref, grad_ref,
    act, cot, up0, up1, dn0, dn1, hid, q_all, load_sem, q_send, q_recv,
    t_part, t_got, t_all, c_all, t_send, t_recv, pre_one,
    s_part, s_core, s_near, s_nrecv, s_far, s_frecv, s_all, s_send, s_recv, full32,
    f_turn, f_near, f_nrecv, f_far, f_frecv, f_send, f_recv, g_part, g_core, g_sum, g_yrecv, g_send, g_recv,
    p_part, p_recv, p_zrecv, p_send, p_recv_sem,
    left, right, score_part,
):
    s = lax.axis_index("section")
    t = lax.axis_index("tensor")
    z, y, c = s // 4, (s // 2) % 2, s % 2

    def section(zz, yy, cc):
        return {"section": zz * 4 + yy * 2 + cc}

    core_peer = section(z, y, 1 - c)
    y_peer = section(z, 1 - y, c)

    def z_at(i):
        far = (i + 1) // 2
        return lax.rem(z + 8 + jnp.where(i % 2 == 0, far, -far), NZ)

    def z_peer(i):
        return section(z_at(i), y, c)

    def t_at(i):
        return t ^ (i + 1)

    def t_peer(i):
        return {"tensor": t_at(i)}

    loads = {}

    def load(name, pairs, slot):
        copies = [pltpu.make_async_copy(a, b, load_sem.at[slot + n]) for n, (a, b) in enumerate(pairs)]
        for one in copies:
            one.start()
        loads[name] = copies

    def ready(name):
        for one in loads.pop(name, ()):
            one.wait()

    def weight(name, ref, buf, slot):
        load(name, [(ref, buf.at[pl.ds(0, H)]), (width_hbm, buf.at[pl.ds(H, K)])], slot)

    load("act", [(act_hbm, act)], 0)
    weight("up0", up_hbm.at[0], up0, 1)
    load("cot", [(cot_hbm, cot)], 3)
    weight("dn1", down_hbm.at[1], dn1, 4)
    weight("dn0", down_hbm.at[0], dn0, 6)
    load("hid", [(hidden_hbm, hid)], 8)
    load("qry", [(query_hbm, q_all.at[z])], 9)
    weight("up1", up_hbm.at[1], up1, 10)

    barrier = pltpu.get_barrier_semaphore()

    def greet(device):
        pl.semaphore_signal(barrier, inc=1, device_id=device, device_id_type=MESH)

    def greet_many(n, peer):
        def one(i, carry):
            greet(peer(i))
            return carry
        lax.fori_loop(0, n, one, 0)

    greet_many(NZ - 1, z_peer)
    greet_many(T - 1, t_peer)
    greet(y_peer)
    greet(core_peer)
    for o in (-2, -1, 1, 2):
        greet(section(lax.rem(z + o + NZ, NZ), 1 - y, c))

    sent = []

    def push(src, dst, peer, send_sem, recv_sem):
        pltpu.make_async_remote_copy(
            src_ref=src, dst_ref=dst, send_sem=send_sem, recv_sem=recv_sem,
            device_id=peer, device_id_type=MESH,
        ).start()

    def fan(n, peer, src, dst, send_sem, recv_sem, whole):
        def one(i, carry):
            push(src(i), dst(i), peer(i), send_sem, recv_sem)
            return carry
        lax.fori_loop(0, n, one, 0, unroll=True)
        sent.append((whole, send_sem))

    def push_one(src, dst, peer, send_sem, recv_sem):
        push(src, dst, peer, send_sem, recv_sem)
        sent.append((dst, send_sem))

    steps = []

    def q_step():
        k = len(steps)
        if k == 0:
            ready("qry")
        for way in range(2):
            if 0 < k and (k < NZ // 2 or way == 0):
                take(q_all.at[0], q_recv.at[way, k - 1])
        steps.append(k)
        if k == NZ // 2:
            return
        for way, sign in enumerate((1, -1)):
            if k < NZ // 2 - 1 or way == 0:
                block = q_all.at[lax.rem(z - sign * k + NZ, NZ)]
                push_one(block, block, section(lax.rem(z + sign + NZ, NZ), y, c), q_send.at[way, k], q_recv.at[way, k])

    rows_of = lambda i, n: pl.ds(pl.multiple_of(i * n, n), n)

    def t_scatter(x, h):
        fan(
            T - 1, t_peer,
            lambda i: t_part.at[x, h, rows_of(t_at(i), B)],
            lambda i: t_got.at[x, h, i],
            t_send.at[0, x, h], t_recv.at[0, x, h], t_got.at[x, h],
        )

    def t_total(x, h):
        take(t_got.at[x, h], t_recv.at[0, x, h])
        total = t_part[x, h, rows_of(t, B), :].astype(F32)
        for i in range(T - 1):
            total += t_got[x, h, i].astype(F32)
        return total

    def t_gather(x, h, buf):
        mine = buf.at[h, rows_of(t, B)]
        others = buf.at[h, pl.ds(0, B * (T - 1))]
        fan(T - 1, t_peer, lambda i: mine, lambda i: mine, t_send.at[1, x, h], t_recv.at[1, x, h], others)
        return others

    near, far = z % 4, z // 4
    hops = [(2, 1), (-1, 1), (1, 1), (2, 0), (-1, 0), (1, 0), (0, 1)]

    def near_of(o, flip):
        zz, yy = lax.rem(z + o + NZ, NZ), (1 - y if flip else y)
        return yy, zz % 4, section(zz, yy, c)

    across = lax.rem(near + 2, 4)
    strides = (6, -6, 2, -2)

    def swap(p, h, value):
        s_part[p, h] = value.astype(BF16)
        full32[h] = value
        push_one(s_part.at[p, h, rows_of(1 - c, M // 2)], s_core.at[p, h], core_peer, s_send.at[0, p, h], s_recv.at[0, p, h])

    def swapped(p, h):
        take(s_core.at[p, h], s_recv.at[0, p, h])
        return full32[h, rows_of(c, M // 2), :] + s_core[p, h].astype(F32)

    def near_start(part, got, send_sem, recv_sem):
        for i, (o, flip) in enumerate(hops):
            yy, zm, peer = near_of(o, flip)
            push(part.at[yy, zm], got.at[i], peer, send_sem, recv_sem)
        sent.append((got, send_sem))

    def near_total(part, got, recv_sem):
        take(got, recv_sem)
        total = part[y, near].astype(F32)
        for i in range(len(hops)):
            total += got[i].astype(F32)
        return total

    half_row = pl.multiple_of(c * (M // 2), M // 2)
    tile_row = pl.multiple_of(half_row + (2 * y + across // 2) * B, B)
    tile_col = pl.multiple_of((across % 2) * (D // 2), D // 2)

    def s_sum(p, h, base):
        value = swapped(p, h)
        part, got = s_near.at[p, h], s_nrecv.at[p, h]
        for yy in range(2):
            for zm in range(4):
                at_row, at_col = (2 * yy + zm // 2) * B, (zm % 2) * (D // 2)
                part[yy, zm] = value[at_row:at_row + B, at_col:at_col + D // 2].astype(BF16)
        near_start(part, got, s_send.at[1, p, h], s_recv.at[1, p, h])
        yield
        s_far[p, h] = near_total(part, got, s_recv.at[1, p, h]).astype(BF16)
        for i, o in enumerate(strides):
            peer = section(lax.rem(z + o + NZ, NZ), y, c)
            push(s_far.at[p, h], s_frecv.at[p, h, i], peer, s_send.at[2, p, h], s_recv.at[2, p, h])
        sent.append((s_frecv.at[p, h], s_send.at[2, p, h]))
        yield
        take(s_frecv.at[p, h], s_recv.at[2, p, h])
        total = s_frecv[p, h, 0].astype(F32)
        for i in range(1, 4):
            total += s_frecv[p, h, i].astype(F32)
        spot = s_all.at[p, h, pl.ds(tile_row, B), pl.ds(tile_col, D // 2)]
        s_all[p, h, pl.ds(tile_row, B), pl.ds(tile_col, D // 2)] = (tile_of(base, h) + total).astype(BF16)
        for o, flip in hops:
            push(spot, spot, near_of(o, flip)[2], s_send.at[3, p, h], s_recv.at[3, p, h])
        sent.append((got, s_send.at[3, p, h]))
        yield
        take(got, s_recv.at[3, p, h])
        half = s_all.at[p, h, pl.ds(half_row, M // 2)]
        push_one(half, half, core_peer, s_send.at[4, p, h], s_recv.at[4, p, h])
        yield
        take(half, s_recv.at[4, p, h])

    def tile_of(ref, h):
        return ref[pl.ds(pl.multiple_of(h * M + tile_row, B), B), pl.ds(tile_col, D // 2)].astype(F32)

    def spread(h):
        q = lax.broadcasted_iota(jnp.int32, (2 * K, K), 0)
        a = lax.broadcasted_iota(jnp.int32, (2 * K, K), 1)
        pick = (a == (q // 8) * 4 + q % 4) & ((q // 4) % 2 == h)
        return jnp.where(pick, 1.0, 0.0).astype(BF16)

    def keep(m, h, value):
        left[m, :, pl.ds(h * M, M)] = against(spread(h), value).astype(BF16)

    def products(m):
        total = dot(left[m], right[m])
        for i in range(16):
            g_part[m // 2, i % 2, (i // 2) % 2, 4 * (m % 2) + i // 4, :, pl.ds(0, K)] = total[8 * i:8 * i + 8]

    def g_swap(u):
        products(2 * u)
        products(2 * u + 1)
        push_one(g_part.at[u, 1 - c], g_core.at[u], core_peer, g_send.at[0, u], g_recv.at[0, u])

    def g_cross(u):
        take(g_core.at[u], g_recv.at[0, u])
        g_sum[u] = g_part[u, c] + g_core[u]
        push_one(g_sum.at[u, 1 - y], g_yrecv.at[u], y_peer, g_send.at[1, u], g_recv.at[1, u])

    at_row = lax.broadcasted_iota(jnp.int32, (8, 4 * K), 0) % 4
    at_lane = lax.broadcasted_iota(jnp.int32, (8, 4 * K), 1) // K

    def g_score(u):
        take(g_yrecv.at[u], g_recv.at[1, u])
        total = jnp.zeros((16, K), F32)
        for i in range(8):
            one = (g_sum[u, y, i] + g_yrecv[u, i])[:, :K]
            wide = jnp.where(at_row == at_lane, jnp.concatenate([one, one, one, one], axis=1), 0.0)
            high = wide.astype(BF16).astype(F32)
            both = jnp.concatenate([high, wide - high], axis=0).astype(BF16)
            total += against(both, q_all[8 * u + i])
        return total

    def stream(h):
        rows = slice(h * M, h * M + M)
        lanes = lax.broadcasted_iota(jnp.int32, (B, W), 1)
        if h == 0:
            ready("act")
            ready("up0")
        t_part[0, h] = against(act[rows], up0[...]).astype(BF16)
        if h == 0:
            pl.semaphore_wait(barrier, NZ - 1 + T - 1 + 2 + 4)
        t_scatter(0, h)
        yield
        if h == 0:
            ready("cot")
            ready("dn1")
        t_part[1, h] = against(cot[rows], dn1[...]).astype(BF16)
        total = t_total(0, h)
        pre_one[h] = total
        t_all[0, h, rows_of(t, B), :] = jnp.where(lanes < H, jax.nn.silu(total), total).astype(BF16)
        others = t_gather(0, h, t_all.at[0])
        yield
        if h == 0:
            ready("dn0")
            ready("hid")
        take(others, t_recv.at[1, 0, h])
        act_one = t_all[0, h, :, pl.ds(0, H)]
        swap(0, h, dot(act_one, dn0[pl.ds(0, H), :]))
        keep(0, h, t_all[0, h, :, pl.ds(H, K)])
        keep(1, h, against(act_one, hid[...]).astype(BF16))
        yield
        going = s_sum(0, h, act)
        next(going)
        t_scatter(1, h)
        yield
        yield from going
        if h == 0:
            ready("up1")
        resid = s_all[0, h]
        t_part[2, h] = against(resid, up1[...]).astype(BF16)
        t_scatter(2, h)
        back = t_total(1, h)
        yield
        total = t_total(2, h)
        act_two = jax.nn.silu(total[:, :H]).astype(BF16)
        own = rows_of(t, B)
        c_all[h, own, pl.ds(0, W)] = jnp.where(lanes < H, back * silu_slope(total), total).astype(BF16)
        c_all[h, own, pl.ds(W, K)] = against(act_two, hid[...]).astype(BF16)
        c_all[h, own, pl.ds(W + K, K)] = back[:, H:].astype(BF16)
        others = t_gather(2, h, c_all)
        yield
        take(others, t_recv.at[1, 2, h])
        delta_two = c_all[h, :, pl.ds(0, H)]
        swap(1, h, dot(delta_two, up1[pl.ds(0, H), :]))
        keep(2, h, c_all[h, :, pl.ds(H, K)])
        keep(3, h, c_all[h, :, pl.ds(W, K)])
        right[3, rows, :] = c_all[h, :, pl.ds(W + K, K)]
        right[2, rows, :] = against(delta_two, hid[...]).astype(BF16)
        yield
        yield from s_sum(1, h, cot)
        t_part[3, h] = against(s_all[1, h], dn0[...]).astype(BF16)
        t_scatter(3, h)
        if h == 1:
            g_swap(1)
        yield
        total = t_total(3, h)
        t_all[1, h, rows_of(t, B), :] = jnp.where(lanes < H, total * silu_slope(pre_one[h]), total).astype(BF16)
        others = t_gather(3, h, t_all.at[1])
        if h == 1:
            g_cross(1)
        yield
        take(others, t_recv.at[1, 3, h])
        delta_one = t_all[1, h, :, pl.ds(0, H)]
        right[1, rows, :] = t_all[1, h, :, pl.ds(H, K)]
        right[0, rows, :] = against(delta_one, hid[...]).astype(BF16)
        if h == 1:
            g_swap(0)
        to = lax.broadcasted_iota(jnp.int32, (M, M), 0)
        came = lax.broadcasted_iota(jnp.int32, (M, M), 1)
        source = (((to // 4) % 2) * 4 + (to // 8) % 4) * 16 + ((to // 32) % 2) * 8 + (to // 64) * 4 + to % 4
        turn = jnp.where(came == source, 1.0, 0.0).astype(BF16)
        turned = dot(turn, delta_one).astype(BF16)
        swap(2, h, dot(turned, up0[pl.ds(0, H), :]))
        if h == 0:
            score_part[...] = g_score(1)
        else:
            g_cross(0)
        yield
        value = swapped(2, h)
        for n in range(16):
            for j in range(8):
                f_turn[h, n, pl.ds(4 * j, 4), :] = value[4 * n:4 * n + 4, 128 * j:128 * j + 128]
        for n in range(8):
            f_near[h, n // 4, (n + 2) % 4] = jnp.concatenate([f_turn[h, 2 * n], f_turn[h, 2 * n + 1]], axis=0).astype(BF16)
        near_start(f_near.at[h], f_nrecv.at[h], f_send.at[h], f_recv.at[h])
        if h == 1:
            scores = score_part[...] + g_score(0)
            p_part[0, :, pl.ds(0, K)] = scores[0:8] + scores[8:16]
            push_one(p_part.at[0], p_recv.at[0], core_peer, p_send.at[0], p_recv_sem.at[0])
        yield
        if h == 1:
            take(p_recv.at[0], p_recv_sem.at[0])
            p_part[1] = p_part[0] + p_recv[0]
            push_one(p_part.at[1], p_recv.at[1], y_peer, p_send.at[1], p_recv_sem.at[1])
        total = near_total(f_near.at[h], f_nrecv.at[h], f_recv.at[h])
        for k in range(2):
            f_far[2 * h + k] = total[32 * k:32 * k + 32].astype(BF16)
            peer = section(4 * (2 * h + k) + across, y, c)
            push(f_far.at[2 * h + k], f_frecv.at[far], peer, f_send.at[2], f_recv.at[2])

    streams = [stream(h) for h in range(EX)]
    g_part[...] = jnp.zeros_like(g_part)
    p_part[...] = jnp.zeros_like(p_part)
    turns = 0
    while streams:
        for one in list(streams):
            try:
                next(one)
            except StopIteration:
                streams.remove(one)
        if turns <= NZ // 2:
            q_step()
        turns += 1

    sent.append((f_frecv, f_send.at[2]))
    take(p_recv.at[1], p_recv_sem.at[1])
    p_part[2] = p_part[1] + p_recv[1]
    fan(NZ - 1, z_peer, lambda i: p_part.at[2], lambda i: p_zrecv.at[i], p_send.at[2], p_recv_sem.at[2], p_zrecv)

    *gone, last = sent
    for whole, sem in gone:
        take(whole, sem)

    take(f_frecv, f_recv.at[2])
    total = f_frecv[0].astype(F32)
    for i in range(1, 4):
        total += f_frecv[i].astype(F32)
    group = s_all[1, z // 8, rows_of(z % 8, 16), :].astype(F32)
    place = 2 * y + c
    own = group[0:4]
    for n in range(1, 4):
        own = jnp.where(place == n, group[4 * n:4 * n + 4], own)
    for j in range(8):
        grad_ref[:, pl.ds(128 * j, 128)] = (own[:, 128 * j:128 * j + 128] + total[4 * j:4 * j + 4]).astype(BF16)

    take(p_zrecv, p_recv_sem.at[2])
    total = p_part[2]
    for i in range(NZ - 1):
        total += p_zrecv[i]
    score_ref[pl.ds(0, 1), :] = jnp.sum(total[0:4, :K], axis=0, keepdims=True)
    score_ref[pl.ds(1, 1), :] = jnp.sum(total[4:8, :K], axis=0, keepdims=True)

    take(*last)


def hand_over(score_in, grad_in, score_ref, grad_ref):
    score_ref[...] = score_in[...]
    grad_ref[...] = grad_in[...]


def on_device(activations, cotangent, up_weight, *others):
    operands = (activations, cotangent, jnp.swapaxes(up_weight, 1, 2)) + others
    dma, vmem = pltpu.SemaphoreType.DMA, pltpu.VMEM
    weight = vmem((W, D), BF16)
    scratch = [
        vmem((EX * M, D), BF16), vmem((EX * M, D), BF16), weight, weight, weight, weight,
        vmem((K, H), BF16), vmem((NZ, K, 4 * K), BF16), dma((12,)), dma((2, NZ // 2)), dma((2, NZ // 2)),
        vmem((4, EX, M, W), BF16), vmem((4, EX, T - 1, B, W), BF16), vmem((2, EX, M, W), BF16), vmem((EX, M, C_WIDTH), BF16),
        dma((2, 4, EX)), dma((2, 4, EX)), vmem((EX, B, W), F32),
        vmem((3, EX, M, D), BF16), vmem((3, EX, M // 2, D), BF16), vmem((2, EX, 2, 4, B, D // 2), BF16), vmem((2, EX, 7, B, D // 2), BF16),
        vmem((2, EX, B, D // 2), BF16), vmem((2, EX, 4, B, D // 2), BF16), vmem((2, EX, M, D), BF16),
        dma((5, 3, EX)), dma((5, 3, EX)), vmem((EX, M, D), F32),
        vmem((EX, 16, 32, 128), F32), vmem((EX, 2, 4, 64, 128), BF16), vmem((EX, 7, 64, 128), BF16),
        vmem((4, 32, 128), BF16), vmem((4, 32, 128), BF16), dma((3,)), dma((3,)),
        vmem((2, 2, 2, 8, 8, 128), F32), vmem((2, 2, 8, 8, 128), F32), vmem((2, 2, 8, 8, 128), F32), vmem((2, 8, 8, 128), F32),
        dma((2, 2)), dma((2, 2)),
        vmem((3, 8, 128), F32), vmem((2, 8, 128), F32), vmem((NZ - 1, 8, 128), F32), dma((3,)), dma((3,)),
        vmem((4, 2 * K, EX * M), BF16), vmem((4, EX * M, K), BF16), vmem((16, K), F32),
    ]
    results = pl.pallas_call(
        kernel,
        name="window",
        out_shape=(jax.ShapeDtypeStruct((EX, K), F32), jax.ShapeDtypeStruct((4, D), BF16)),
        in_specs=[pl.BlockSpec(memory_space=pltpu.HBM)] * 7,
        out_specs=(pl.BlockSpec(memory_space=pltpu.VMEM), pl.BlockSpec(memory_space=pltpu.VMEM)),
        scratch_shapes=scratch,
        compiler_params=pltpu.CompilerParams(collective_id=0, has_side_effects=True, vmem_limit_bytes=60 << 20),
        cost_estimate=pl.CostEstimate(flops=2 * 10**9, bytes_accessed=5 * 10**6, transcendentals=0),
    )(*operands)
    whole = [pl.BlockSpec(memory_space=pltpu.VMEM)] * 2
    return pl.pallas_call(
        hand_over,
        name="hand_over",
        out_shape=tuple(jax.ShapeDtypeStruct(r.shape, r.dtype) for r in results),
        in_specs=whole,
        out_specs=tuple(whole),
    )(*results)


def solution(mesh):
    placed = (
        P(None, "tensor"),
        P(None, "tensor"),
        P(None, "tensor", "section"),
        P(None, "section", "tensor"),
        P(None, "tensor"),
        P(None, "section"),
        P("tensor", "section"),
    )
    return jax.shard_map(
        on_device,
        mesh=mesh,
        in_specs=placed,
        out_specs=(P(None, "tensor"), P("section", "tensor")),
        check_vma=False,
    )
```

```python
import functools

import jax
import jax.numpy as jnp
from jax import lax
from jax.experimental import pallas as pl
from jax.experimental.pallas import tpu as pltpu
from jax.sharding import PartitionSpec as P

MESH = pl.DeviceIdType.MESH
F32, BF16 = jnp.float32, jnp.bfloat16
EX = 2
M = 128
T = 8
NZ = 16
B = M // T
D = 1024
H = 448
K = 64
W = H + K
C_WIDTH = W + 2 * K


def silu_slope(values):
    sigma = jax.nn.sigmoid(values)
    return sigma * (1.0 + values * (1.0 - sigma))


def dot(a, b):
    return jnp.dot(a, b, preferred_element_type=F32)


def against(a, b):
    return lax.dot_general(a, b, (((1,), (1,)), ((), ())), preferred_element_type=F32)


def take(ref, sem):
    pltpu.make_async_copy(ref, ref, sem).wait()


def kernel(
    act_hbm, cot_hbm, up_hbm, down_hbm, width_hbm, hidden_hbm, query_hbm,
    score_ref, grad_ref,
    act, cot, up0, up1, dn0, dn1, hid, q_all, load_sem, q_send, q_recv,
    t_part, t_got, t_all, c_all, t_send, t_recv, pre_one,
    s_part, s_core, s_near, s_nrecv, s_far, s_frecv, s_all, s_send, s_recv, full32,
    f_turn, f_near, f_nrecv, f_far, f_frecv, f_send, f_recv, g_part, g_core, g_sum, g_yrecv, g_send, g_recv,
    p_part, p_recv, p_zrecv, p_send, p_recv_sem,
    left, right, score_part,
):
    s = lax.axis_index("section")
    t = lax.axis_index("tensor")
    z, y, c = s // 4, (s // 2) % 2, s % 2

    def section(zz, yy, cc):
        return {"section": zz * 4 + yy * 2 + cc}

    core_peer = section(z, y, 1 - c)
    y_peer = section(z, 1 - y, c)

    def z_at(i):
        far = (i + 1) // 2
        return lax.rem(z + 8 + jnp.where(i % 2 == 0, far, -far), NZ)

    def z_peer(i):
        return section(z_at(i), y, c)

    def t_at(i):
        return t ^ (i + 1)

    def t_peer(i):
        return {"tensor": t_at(i)}

    loads = {}

    def load(name, pairs, slot):
        copies = [pltpu.make_async_copy(a, b, load_sem.at[slot + n]) for n, (a, b) in enumerate(pairs)]
        for one in copies:
            one.start()
        loads[name] = copies

    def ready(name):
        for one in loads.pop(name, ()):
            one.wait()

    def weight(name, ref, buf, slot):
        load(name, [(ref, buf.at[pl.ds(0, H)]), (width_hbm, buf.at[pl.ds(H, K)])], slot)

    load("act", [(act_hbm, act)], 0)
    weight("up0", up_hbm.at[0], up0, 1)
    load("cot", [(cot_hbm, cot)], 3)
    weight("dn1", down_hbm.at[1], dn1, 4)
    weight("dn0", down_hbm.at[0], dn0, 6)
    load("hid", [(hidden_hbm, hid)], 8)
    load("qry", [(query_hbm, q_all.at[z])], 9)
    weight("up1", up_hbm.at[1], up1, 10)

    barrier = pltpu.get_barrier_semaphore()

    def greet(device):
        pl.semaphore_signal(barrier, inc=1, device_id=device, device_id_type=MESH)

    def greet_many(n, peer):
        def one(i, carry):
            greet(peer(i))
            return carry
        lax.fori_loop(0, n, one, 0)

    greet_many(NZ - 1, z_peer)
    greet_many(T - 1, t_peer)
    greet(y_peer)
    greet(core_peer)
    for o in (-2, -1, 1, 2):
        greet(section(lax.rem(z + o + NZ, NZ), 1 - y, c))

    sent = []

    def push(src, dst, peer, send_sem, recv_sem):
        pltpu.make_async_remote_copy(
            src_ref=src, dst_ref=dst, send_sem=send_sem, recv_sem=recv_sem,
            device_id=peer, device_id_type=MESH,
        ).start()

    def fan(n, peer, src, dst, send_sem, recv_sem, whole):
        def one(i, carry):
            push(src(i), dst(i), peer(i), send_sem, recv_sem)
            return carry
        lax.fori_loop(0, n, one, 0, unroll=True)
        sent.append((whole, send_sem))

    def push_one(src, dst, peer, send_sem, recv_sem):
        push(src, dst, peer, send_sem, recv_sem)
        sent.append((dst, send_sem))

    steps = []

    def q_step():
        k = len(steps)
        if k == 0:
            ready("qry")
        for way in range(2):
            if 0 < k and (k < NZ // 2 or way == 0):
                take(q_all.at[0], q_recv.at[way, k - 1])
        steps.append(k)
        if k == NZ // 2:
            return
        for way, sign in enumerate((1, -1)):
            if k < NZ // 2 - 1 or way == 0:
                block = q_all.at[lax.rem(z - sign * k + NZ, NZ)]
                push_one(block, block, section(lax.rem(z + sign + NZ, NZ), y, c), q_send.at[way, k], q_recv.at[way, k])

    rows_of = lambda i, n: pl.ds(pl.multiple_of(i * n, n), n)

    def t_scatter(x, h):
        fan(
            T - 1, t_peer,
            lambda i: t_part.at[x, h, rows_of(t_at(i), B)],
            lambda i: t_got.at[x, h, i],
            t_send.at[0, x, h], t_recv.at[0, x, h], t_got.at[x, h],
        )

    def t_total(x, h):
        take(t_got.at[x, h], t_recv.at[0, x, h])
        total = t_part[x, h, rows_of(t, B), :].astype(F32)
        for i in range(T - 1):
            total += t_got[x, h, i].astype(F32)
        return total

    def t_gather(x, h, buf):
        mine = buf.at[h, rows_of(t, B)]
        others = buf.at[h, pl.ds(0, B * (T - 1))]
        fan(T - 1, t_peer, lambda i: mine, lambda i: mine, t_send.at[1, x, h], t_recv.at[1, x, h], others)
        return others

    near, far = z % 4, z // 4
    hops = [(2, 1), (-1, 1), (1, 1), (2, 0), (-1, 0), (1, 0), (0, 1)]

    def near_of(o, flip):
        zz, yy = lax.rem(z + o + NZ, NZ), (1 - y if flip else y)
        return yy, zz % 4, section(zz, yy, c)

    across = lax.rem(near + 2, 4)
    strides = (6, -6, 2, -2)

    def swap(p, h, value):
        s_part[p, h] = value.astype(BF16)
        full32[h] = value
        push_one(s_part.at[p, h, rows_of(1 - c, M // 2)], s_core.at[p, h], core_peer, s_send.at[0, p, h], s_recv.at[0, p, h])

    def swapped(p, h):
        take(s_core.at[p, h], s_recv.at[0, p, h])
        return full32[h, rows_of(c, M // 2), :] + s_core[p, h].astype(F32)

    def near_start(part, got, send_sem, recv_sem):
        for i, (o, flip) in enumerate(hops):
            yy, zm, peer = near_of(o, flip)
            push(part.at[yy, zm], got.at[i], peer, send_sem, recv_sem)
        sent.append((got, send_sem))

    def near_total(part, got, recv_sem):
        take(got, recv_sem)
        total = part[y, near].astype(F32)
        for i in range(len(hops)):
            total += got[i].astype(F32)
        return total

    half_row = pl.multiple_of(c * (M // 2), M // 2)
    tile_row = pl.multiple_of(half_row + (2 * y + across // 2) * B, B)
    tile_col = pl.multiple_of((across % 2) * (D // 2), D // 2)

    def s_sum(p, h, base):
        value = swapped(p, h)
        part, got = s_near.at[p, h], s_nrecv.at[p, h]
        for yy in range(2):
            for zm in range(4):
                at_row, at_col = (2 * yy + zm // 2) * B, (zm % 2) * (D // 2)
                part[yy, zm] = value[at_row:at_row + B, at_col:at_col + D // 2].astype(BF16)
        near_start(part, got, s_send.at[1, p, h], s_recv.at[1, p, h])
        yield
        s_far[p, h] = near_total(part, got, s_recv.at[1, p, h]).astype(BF16)
        for i, o in enumerate(strides):
            peer = section(lax.rem(z + o + NZ, NZ), y, c)
            push(s_far.at[p, h], s_frecv.at[p, h, i], peer, s_send.at[2, p, h], s_recv.at[2, p, h])
        sent.append((s_frecv.at[p, h], s_send.at[2, p, h]))
        yield
        take(s_frecv.at[p, h], s_recv.at[2, p, h])
        total = s_frecv[p, h, 0].astype(F32)
        for i in range(1, 4):
            total += s_frecv[p, h, i].astype(F32)
        spot = s_all.at[p, h, pl.ds(tile_row, B), pl.ds(tile_col, D // 2)]
        s_all[p, h, pl.ds(tile_row, B), pl.ds(tile_col, D // 2)] = (tile_of(base, h) + total).astype(BF16)
        for o, flip in hops:
            push(spot, spot, near_of(o, flip)[2], s_send.at[3, p, h], s_recv.at[3, p, h])
        sent.append((got, s_send.at[3, p, h]))
        yield
        take(got, s_recv.at[3, p, h])
        half = s_all.at[p, h, pl.ds(half_row, M // 2)]
        push_one(half, half, core_peer, s_send.at[4, p, h], s_recv.at[4, p, h])
        yield
        take(half, s_recv.at[4, p, h])

    def tile_of(ref, h):
        return ref[pl.ds(pl.multiple_of(h * M + tile_row, B), B), pl.ds(tile_col, D // 2)].astype(F32)

    def spread(h):
        q = lax.broadcasted_iota(jnp.int32, (2 * K, K), 0)
        a = lax.broadcasted_iota(jnp.int32, (2 * K, K), 1)
        pick = (a == (q // 8) * 4 + q % 4) & ((q // 4) % 2 == h)
        return jnp.where(pick, 1.0, 0.0).astype(BF16)

    def keep(m, h, value):
        left[m, :, pl.ds(h * M, M)] = against(spread(h), value).astype(BF16)

    def products(m):
        total = dot(left[m], right[m])
        for i in range(16):
            g_part[m // 2, i % 2, (i // 2) % 2, 4 * (m % 2) + i // 4, :, pl.ds(0, K)] = total[8 * i:8 * i + 8]

    def g_swap(u):
        products(2 * u)
        products(2 * u + 1)
        push_one(g_part.at[u, 1 - c], g_core.at[u], core_peer, g_send.at[0, u], g_recv.at[0, u])

    def g_cross(u):
        take(g_core.at[u], g_recv.at[0, u])
        g_sum[u] = g_part[u, c] + g_core[u]
        push_one(g_sum.at[u, 1 - y], g_yrecv.at[u], y_peer, g_send.at[1, u], g_recv.at[1, u])

    at_row = lax.broadcasted_iota(jnp.int32, (8, 4 * K), 0) % 4
    at_lane = lax.broadcasted_iota(jnp.int32, (8, 4 * K), 1) // K

    def g_score(u):
        take(g_yrecv.at[u], g_recv.at[1, u])
        total = jnp.zeros((16, K), F32)
        for i in range(8):
            one = (g_sum[u, y, i] + g_yrecv[u, i])[:, :K]
            wide = jnp.where(at_row == at_lane, jnp.concatenate([one, one, one, one], axis=1), 0.0)
            high = wide.astype(BF16).astype(F32)
            both = jnp.concatenate([high, wide - high], axis=0).astype(BF16)
            total += against(both, q_all[8 * u + i])
        return total

    def stream(h):
        rows = slice(h * M, h * M + M)
        lanes = lax.broadcasted_iota(jnp.int32, (B, W), 1)
        if h == 0:
            ready("act")
            ready("up0")
        t_part[0, h] = against(act[rows], up0[...]).astype(BF16)
        if h == 0:
            pl.semaphore_wait(barrier, NZ - 1 + T - 1 + 2 + 4)
        t_scatter(0, h)
        yield
        if h == 0:
            ready("cot")
            ready("dn1")
        t_part[1, h] = against(cot[rows], dn1[...]).astype(BF16)
        total = t_total(0, h)
        pre_one[h] = total
        t_all[0, h, rows_of(t, B), :] = jnp.where(lanes < H, jax.nn.silu(total), total).astype(BF16)
        others = t_gather(0, h, t_all.at[0])
        yield
        if h == 0:
            ready("dn0")
            ready("hid")
        take(others, t_recv.at[1, 0, h])
        act_one = t_all[0, h, :, pl.ds(0, H)]
        swap(0, h, dot(act_one, dn0[pl.ds(0, H), :]))
        keep(0, h, t_all[0, h, :, pl.ds(H, K)])
        keep(1, h, against(act_one, hid[...]).astype(BF16))
        yield
        going = s_sum(0, h, act)
        next(going)
        t_scatter(1, h)
        yield
        yield from going
        if h == 0:
            ready("up1")
        resid = s_all[0, h]
        t_part[2, h] = against(resid, up1[...]).astype(BF16)
        t_scatter(2, h)
        back = t_total(1, h)
        yield
        total = t_total(2, h)
        act_two = jax.nn.silu(total[:, :H]).astype(BF16)
        own = rows_of(t, B)
        c_all[h, own, pl.ds(0, W)] = jnp.where(lanes < H, back * silu_slope(total), total).astype(BF16)
        c_all[h, own, pl.ds(W, K)] = against(act_two, hid[...]).astype(BF16)
        c_all[h, own, pl.ds(W + K, K)] = back[:, H:].astype(BF16)
        others = t_gather(2, h, c_all)
        yield
        take(others, t_recv.at[1, 2, h])
        delta_two = c_all[h, :, pl.ds(0, H)]
        swap(1, h, dot(delta_two, up1[pl.ds(0, H), :]))
        keep(2, h, c_all[h, :, pl.ds(H, K)])
        keep(3, h, c_all[h, :, pl.ds(W, K)])
        right[3, rows, :] = c_all[h, :, pl.ds(W + K, K)]
        right[2, rows, :] = against(delta_two, hid[...]).astype(BF16)
        yield
        yield from s_sum(1, h, cot)
        t_part[3, h] = against(s_all[1, h], dn0[...]).astype(BF16)
        t_scatter(3, h)
        if h == 1:
            g_swap(1)
        yield
        total = t_total(3, h)
        t_all[1, h, rows_of(t, B), :] = jnp.where(lanes < H, total * silu_slope(pre_one[h]), total).astype(BF16)
        others = t_gather(3, h, t_all.at[1])
        if h == 1:
            g_cross(1)
            score_part[...] = g_score(1)
        yield
        take(others, t_recv.at[1, 3, h])
        delta_one = t_all[1, h, :, pl.ds(0, H)]
        right[1, rows, :] = t_all[1, h, :, pl.ds(H, K)]
        right[0, rows, :] = against(delta_one, hid[...]).astype(BF16)
        if h == 1:
            g_swap(0)
        to = lax.broadcasted_iota(jnp.int32, (M, M), 0)
        came = lax.broadcasted_iota(jnp.int32, (M, M), 1)
        source = (((to // 4) % 2) * 4 + (to // 8) % 4) * 16 + ((to // 32) % 2) * 8 + (to // 64) * 4 + to % 4
        turn = jnp.where(came == source, 1.0, 0.0).astype(BF16)
        turned = dot(turn, delta_one).astype(BF16)
        swap(2, h, dot(turned, up0[pl.ds(0, H), :]))
        if h == 1:
            g_cross(0)
        yield
        value = swapped(2, h)
        for n in range(16):
            for j in range(8):
                f_turn[h, n, pl.ds(4 * j, 4), :] = value[4 * n:4 * n + 4, 128 * j:128 * j + 128]
        for n in range(8):
            f_near[h, n // 4, (n + 2) % 4] = jnp.concatenate([f_turn[h, 2 * n], f_turn[h, 2 * n + 1]], axis=0).astype(BF16)
        near_start(f_near.at[h], f_nrecv.at[h], f_send.at[h], f_recv.at[h])
        if h == 1:
            scores = score_part[...] + g_score(0)
            p_part[0, :, pl.ds(0, K)] = scores[0:8] + scores[8:16]
            push_one(p_part.at[0], p_recv.at[0], core_peer, p_send.at[0], p_recv_sem.at[0])
        yield
        if h == 1:
            take(p_recv.at[0], p_recv_sem.at[0])
            p_part[1] = p_part[0] + p_recv[0]
            push_one(p_part.at[1], p_recv.at[1], y_peer, p_send.at[1], p_recv_sem.at[1])
        total = near_total(f_near.at[h], f_nrecv.at[h], f_recv.at[h])
        for k in range(2):
            f_far[2 * h + k] = total[32 * k:32 * k + 32].astype(BF16)
            peer = section(4 * (2 * h + k) + across, y, c)
            push(f_far.at[2 * h + k], f_frecv.at[far], peer, f_send.at[2], f_recv.at[2])

    streams = [stream(h) for h in range(EX)]
    g_part[...] = jnp.zeros_like(g_part)
    p_part[...] = jnp.zeros_like(p_part)
    turns = 0
    while streams:
        for one in list(streams):
            try:
                next(one)
            except StopIteration:
                streams.remove(one)
        if turns <= NZ // 2:
            q_step()
        turns += 1

    sent.append((f_frecv, f_send.at[2]))
    take(p_recv.at[1], p_recv_sem.at[1])
    p_part[2] = p_part[1] + p_recv[1]
    fan(NZ - 1, z_peer, lambda i: p_part.at[2], lambda i: p_zrecv.at[i], p_send.at[2], p_recv_sem.at[2], p_zrecv)

    *gone, last = sent
    for whole, sem in gone:
        take(whole, sem)

    take(f_frecv, f_recv.at[2])
    total = f_frecv[0].astype(F32)
    for i in range(1, 4):
        total += f_frecv[i].astype(F32)
    group = s_all[1, z // 8, rows_of(z % 8, 16), :].astype(F32)
    place = 2 * y + c
    own = group[0:4]
    for n in range(1, 4):
        own = jnp.where(place == n, group[4 * n:4 * n + 4], own)
    for j in range(8):
        grad_ref[:, pl.ds(128 * j, 128)] = (own[:, 128 * j:128 * j + 128] + total[4 * j:4 * j + 4]).astype(BF16)

    take(p_zrecv, p_recv_sem.at[2])
    total = p_part[2]
    for i in range(NZ - 1):
        total += p_zrecv[i]
    score_ref[pl.ds(0, 1), :] = jnp.sum(total[0:4, :K], axis=0, keepdims=True)
    score_ref[pl.ds(1, 1), :] = jnp.sum(total[4:8, :K], axis=0, keepdims=True)

    take(*last)


def hand_over(score_in, grad_in, score_ref, grad_ref):
    score_ref[...] = score_in[...]
    grad_ref[...] = grad_in[...]


def on_device(activations, cotangent, up_weight, *others):
    operands = (activations, cotangent, jnp.swapaxes(up_weight, 1, 2)) + others
    dma, vmem = pltpu.SemaphoreType.DMA, pltpu.VMEM
    weight = vmem((W, D), BF16)
    scratch = [
        vmem((EX * M, D), BF16), vmem((EX * M, D), BF16), weight, weight, weight, weight,
        vmem((K, H), BF16), vmem((NZ, K, 4 * K), BF16), dma((12,)), dma((2, NZ // 2)), dma((2, NZ // 2)),
        vmem((4, EX, M, W), BF16), vmem((4, EX, T - 1, B, W), BF16), vmem((2, EX, M, W), BF16), vmem((EX, M, C_WIDTH), BF16),
        dma((2, 4, EX)), dma((2, 4, EX)), vmem((EX, B, W), F32),
        vmem((3, EX, M, D), BF16), vmem((3, EX, M // 2, D), BF16), vmem((2, EX, 2, 4, B, D // 2), BF16), vmem((2, EX, 7, B, D // 2), BF16),
        vmem((2, EX, B, D // 2), BF16), vmem((2, EX, 4, B, D // 2), BF16), vmem((2, EX, M, D), BF16),
        dma((5, 3, EX)), dma((5, 3, EX)), vmem((EX, M, D), F32),
        vmem((EX, 16, 32, 128), F32), vmem((EX, 2, 4, 64, 128), BF16), vmem((EX, 7, 64, 128), BF16),
        vmem((4, 32, 128), BF16), vmem((4, 32, 128), BF16), dma((3,)), dma((3,)),
        vmem((2, 2, 2, 8, 8, 128), F32), vmem((2, 2, 8, 8, 128), F32), vmem((2, 2, 8, 8, 128), F32), vmem((2, 8, 8, 128), F32),
        dma((2, 2)), dma((2, 2)),
        vmem((3, 8, 128), F32), vmem((2, 8, 128), F32), vmem((NZ - 1, 8, 128), F32), dma((3,)), dma((3,)),
        vmem((4, 2 * K, EX * M), BF16), vmem((4, EX * M, K), BF16), vmem((16, K), F32),
    ]
    results = pl.pallas_call(
        kernel,
        name="window",
        out_shape=(jax.ShapeDtypeStruct((EX, K), F32), jax.ShapeDtypeStruct((4, D), BF16)),
        in_specs=[pl.BlockSpec(memory_space=pltpu.HBM)] * 7,
        out_specs=(pl.BlockSpec(memory_space=pltpu.VMEM), pl.BlockSpec(memory_space=pltpu.VMEM)),
        scratch_shapes=scratch,
        compiler_params=pltpu.CompilerParams(collective_id=0, has_side_effects=True, vmem_limit_bytes=60 << 20),
        cost_estimate=pl.CostEstimate(flops=2 * 10**9, bytes_accessed=5 * 10**6, transcendentals=0),
    )(*operands)
    whole = [pl.BlockSpec(memory_space=pltpu.VMEM)] * 2
    return pl.pallas_call(
        hand_over,
        name="hand_over",
        out_shape=tuple(jax.ShapeDtypeStruct(r.shape, r.dtype) for r in results),
        in_specs=whole,
        out_specs=tuple(whole),
    )(*results)


def solution(mesh):
    placed = (
        P(None, "tensor"),
        P(None, "tensor"),
        P(None, "tensor", "section"),
        P(None, "section", "tensor"),
        P(None, "tensor"),
        P(None, "section"),
        P("tensor", "section"),
    )
    return jax.shard_map(
        on_device,
        mesh=mesh,
        in_specs=placed,
        out_specs=(P(None, "tensor"), P("section", "tensor")),
        check_vma=False,
    )
```
